256 devices in a mesh: row: 16 (over z_hi, y), col: 16 (over x, z_lo, core).
Axes of the slice: x: 4, y: 4, z: 8 (z_hi: 4, z_lo: 2; z = z_hi * 2 + z_lo), core: 2. Of those that a mesh axis runs over, the one named last changes fastest.
Arguments:
- object_field: float32 [2, 8192, 8192], P(None, 'row', 'col'), may hold values from -6 to 6
- probe: float32 [2, 2, 256, 256], replicated, may hold values from -6 to 6
- own_pos: int32 [1024, 2], P(('row', 'col')), may hold values from 0 to 7936, as said below
- own_amp: bfloat16 [1024, 256, 256], P(('row', 'col')), may hold values from 0 to 4
- lend_pos: int32 [512, 2], P(('row', 'col')), may hold values from 0 to 7936, as said below
- lend_live: int32 [512], P(('row', 'col')), may hold values from 0 to 1, as said below
- recv_amp: bfloat16 [512, 256, 256], P(('row', 'col')), may hold values from 0 to 4
Outputs:
- new_object: float32 [2, 8192, 8192], P(None, 'row', 'col')
- probe_grad: float32 [2, 2, 256, 256], replicated
The draws below stay inside these ranges and needn't reach their ends.
Inputs may be any that keep to these rules, and one draw needn't show every extreme that they name: `own_pos`: each frame of tile (i, j) lies inside the object and its offset is at most 128 before the tile's first pixel and at most 384 after it, along both dimensions. `lend_pos`: offsets as for own_pos, relative to the lending tile, also where the slot is empty. `lend_live`: slots to the next column are 0 in the last tile column, slots to the previous column are 0 in the first.
All inputs are finite; a program needn't handle non-finite values.
Results may differ from the reference program's by a relative error of at most 0.00045.
Values may be sent and summed in bfloat16 or wider, within the bound.
A program may use at most 128 MiB of HBM per device.

```python
import math
import jax
import jax.numpy as jnp
from jax import lax

FR = 256
MODES = 2
TILE = 512
OWN_DEV = 4
LCAP = 1
NR = 8192
NC = 8192
OWN_ALL = 1024
LEND_ALL = 512
N_ROW = 16
N_COL = 16


def frame_offsets(key, count, per_device):
    device_index = jnp.arange(count, dtype=jnp.int32) // per_device
    tile_row = device_index // N_COL
    tile_col = device_index % N_COL
    half_width = FR // 2
    low_row = jnp.maximum(tile_row * TILE - half_width, 0)
    high_row = jnp.minimum(tile_row * TILE + TILE - half_width, NR - FR)
    low_col = jnp.maximum(tile_col * TILE - half_width, 0)
    high_col = jnp.minimum(tile_col * TILE + TILE - half_width, NC - FR)
    key_rows, key_cols = jax.random.split(key)
    rows_drawn = jax.random.randint(key_rows, (count,), low_row, high_row + 1)
    cols_drawn = jax.random.randint(key_cols, (count,), low_col, high_col + 1)
    rows_drawn = rows_drawn.at[0].set(low_row[0]).at[count - 1].set(high_row[count - 1])
    cols_drawn = cols_drawn.at[0].set(low_col[0]).at[count - 1].set(high_col[count - 1])
    return jnp.stack([rows_drawn, cols_drawn], axis=1).astype(jnp.int32)


def draw_own_pos(key, part):
    key = jax.random.fold_in(key, 11)
    return frame_offsets(key, OWN_ALL, OWN_DEV)


def draw_lend_pos(key, part):
    key = jax.random.fold_in(key, 12)
    return frame_offsets(key, LEND_ALL, 2 * LCAP)


def draw_lend_live(key, part):
    key = jax.random.fold_in(key, 13)
    slot_index = jnp.arange(LEND_ALL, dtype=jnp.int32)
    device_index = slot_index // (2 * LCAP)
    tile_col = device_index % N_COL
    heading = slot_index // LCAP % 2
    allowed = jnp.where(heading == 0, tile_col < N_COL - 1, tile_col > 0).astype(jnp.int32)
    coins = jax.random.randint(key, (LEND_ALL,), 0, 2)
    live = coins * allowed
    return live.at[0].set(1).astype(jnp.int32)


def levels(key, dims, shards, low, high):
    def one(axis_at, shards_of):
        heights = jax.random.uniform(jax.random.fold_in(jax.random.fold_in(key, 6), axis_at), (shards_of,), jnp.float32, low / len(shards), high / len(shards))
        return jnp.repeat(jnp.exp(heights), dims[axis_at] // shards_of).reshape((-1,) + (1,) * (len(dims) - axis_at - 1))

    loudness = one(*shards[0])
    for cut in shards[1:]:
        loudness = loudness * one(*cut)
    return loudness


def centred(key, extent, deviation, reach, shards=(), held_as=jnp.bfloat16):
    drawn = jax.random.normal(key, extent, jnp.float32) * deviation
    if len(shards) > 0:
        drawn = levels(key, extent, shards, -0.22, 0.18) * drawn
    return jnp.clip(drawn, min=-reach, max=reach).astype(held_as)


def setup_inputs(seed: int = 0) -> dict:
    key_of = jax.random.split(jax.random.key(seed), 8)
    object_field = centred(key_of[0], (2, NR, NC), 1.0, 6.0, ((1, 16), (2, 16)), jnp.float32)
    probe = centred(key_of[1], (MODES, 2, FR, FR), 1.0, 6.0, (), jnp.float32)
    own_pos = draw_own_pos(jax.random.fold_in(key_of[7], 71), 0)
    own_amp = jnp.clip(4.0 * jax.random.uniform(key_of[3], (OWN_ALL, FR, FR), jnp.float32) ** levels(key_of[3], (OWN_ALL, FR, FR), ((0, 256),), -0.2, 0.2), 0.0, 4.0).astype(jnp.bfloat16)
    lend_pos = draw_lend_pos(jax.random.fold_in(key_of[7], 71), 0)
    lend_live = draw_lend_live(jax.random.fold_in(key_of[7], 71), 0)
    recv_amp = jnp.clip(4.0 * jax.random.uniform(key_of[6], (LEND_ALL, FR, FR), jnp.float32) ** levels(key_of[6], (LEND_ALL, FR, FR), ((0, 256),), -0.2, 0.2), 0.0, 4.0).astype(jnp.bfloat16)
    return {"object_field": object_field, "probe": probe, "own_pos": own_pos, "own_amp": own_amp, "lend_pos": lend_pos, "lend_live": lend_live, "recv_amp": recv_amp}


highest_precision = lax.Precision.HIGHEST

def dft_tables(length):
    counter = jnp.arange(length, dtype=jnp.int32)
    product = counter[:, None] * counter[None, :] % length
    angles = product.astype(jnp.float32) * (2.0 * math.pi / length)
    scaling = 1.0 / math.sqrt(length)
    return (jnp.cos(angles) * scaling, jnp.sin(angles) * scaling)

def left_product(table, values):
    return jnp.einsum('kn,...nm->...km', table, values, precision=highest_precision)

def right_product(values, table):
    return jnp.einsum('...kn,nm->...km', values, table, precision=highest_precision)

def transform(real_part, imag_part, cosine, sine, direction):
    left_real = left_product(cosine, real_part) - direction * left_product(sine, imag_part)
    left_imag = left_product(cosine, imag_part) + direction * left_product(sine, real_part)
    out_real = right_product(left_real, cosine) - direction * right_product(left_imag, sine)
    out_imag = right_product(left_imag, cosine) + direction * right_product(left_real, sine)
    return (out_real, out_imag)

def frame_terms(patches, amplitudes, probe, cosine, sine):
    probe_real = probe[:, 0][None]
    probe_imag = probe[:, 1][None]
    patch_real = patches[:, 0][:, None]
    patch_imag = patches[:, 1][:, None]
    exit_real = probe_real * patch_real - probe_imag * patch_imag
    exit_imag = probe_real * patch_imag + probe_imag * patch_real
    far_real, far_imag = transform(exit_real, exit_imag, cosine, sine, -1.0)
    power = lax.optimization_barrier(jnp.sum(far_real * far_real + far_imag * far_imag, axis=1))
    ratio = amplitudes.astype(jnp.float32) / jnp.maximum(jnp.sqrt(power), 1.0)
    keeping = (1.0 - ratio)[:, None]
    back_real, back_imag = transform(far_real * keeping, far_imag * keeping, cosine, sine, 1.0)
    object_real = lax.optimization_barrier(jnp.sum(probe_real * back_real + probe_imag * back_imag, axis=1))
    object_imag = lax.optimization_barrier(jnp.sum(probe_real * back_imag - probe_imag * back_real, axis=1))
    grad_real = lax.optimization_barrier(jnp.sum(patch_real * back_real + patch_imag * back_imag, axis=0))
    grad_imag = lax.optimization_barrier(jnp.sum(patch_real * back_imag - patch_imag * back_real, axis=0))
    return (jnp.stack([object_real, object_imag], axis=1), jnp.stack([grad_real, grad_imag], axis=1))

def reference(object_field, probe, own_pos, own_amp, lend_pos, lend_live, recv_amp):
    cosine, sine = dft_tables(FR)
    arranged = recv_amp.reshape(N_ROW, N_COL, 2, LCAP, FR, FR)
    to_right = jnp.roll(arranged[:, :, 0], -1, axis=1)
    to_left = jnp.roll(arranged[:, :, 1], 1, axis=1)
    lent_amp = jnp.stack([to_right, to_left], axis=2).reshape(LEND_ALL, FR, FR)
    positions = jnp.concatenate([own_pos, lend_pos], axis=0).astype(jnp.int32)
    amplitudes = jnp.concatenate([own_amp, lent_amp], axis=0)
    weights = jnp.concatenate([jnp.ones((OWN_ALL,), jnp.float32), lend_live.astype(jnp.float32)])
    anchor = jnp.zeros((), jnp.int32)

    def visit(slot_index, carry):
        object_grad, probe_sum = carry
        row_start = positions[slot_index, 0]
        col_start = positions[slot_index, 1]
        corner_start = (anchor, row_start, col_start)
        patch = lax.dynamic_slice(object_field, corner_start, (2, FR, FR)) * weights[slot_index]
        amplitude = lax.dynamic_index_in_dim(amplitudes, slot_index, 0, keepdims=True)
        object_term, probe_term = frame_terms(patch[None], amplitude, probe, cosine, sine)
        current = lax.dynamic_slice(object_grad, corner_start, (2, FR, FR))
        object_grad = lax.dynamic_update_slice(object_grad, current + object_term[0], corner_start)
        return (object_grad, probe_sum + probe_term)
    initial = (jnp.zeros_like(object_field), jnp.zeros_like(probe))
    object_grad, probe_sum = lax.fori_loop(0, OWN_ALL + LEND_ALL, visit, initial)
    peak = jnp.max(lax.optimization_barrier(jnp.sum(probe * probe, axis=(0, 1)))) + 1e-06
    new_object = object_field - object_grad / peak
    probe_grad = probe_sum / OWN_ALL
    return (new_object, probe_grad)
```

```python
import math

import jax
import jax.numpy as jnp
import ml_dtypes
import numpy as np
from jax import lax
from jax.experimental import pallas as pl
from jax.experimental.pallas import tpu as pltpu
from jax.sharding import PartitionSpec as P

MESH = pl.DeviceIdType.MESH
FR = 256
H = 128
TILE = 512
WIN = 768
OWN = 4
FRAMES = 6
F32 = jnp.float32
BF = jnp.bfloat16
I16 = jnp.int16

HALF = 4 * H + 16
STRIP = 8 * H + 16
CORNER = 2 * H + 16
PIECE = 64 + 16


def at_in(k):
    if k < 4:
        return k * HALF, HALF
    if k < 6:
        return 4 * HALF + (k - 4) * STRIP, STRIP
    return 4 * HALF + 2 * STRIP + (k - 6) * CORNER, CORNER


def view(ref, k):
    start, size = at_in(k)
    return ref.at[pl.ds(start, size)]


OUT_ROWS = 4 * HALF + 2 * STRIP
IN_ROWS = OUT_ROWS + 4 * CORNER


def code_of(largest):
    octaves = jnp.log(jnp.maximum(largest, 1e-30)) * (1.0 / math.log(2.0))
    return jnp.floor(16.0 * (14.98 - octaves))


def scale_of(code):
    return jnp.exp(code * (math.log(2.0) / 16.0))


def tall(tile, rows):
    return jnp.concatenate([tile] * (rows // 16), axis=0)


def encode(ref, places, values, code_at):
    largest = None
    for v in values:
        for t in range(0, v.shape[0], 16):
            a = jnp.abs(v[t : t + 16])
            largest = a if largest is None else jnp.maximum(largest, a)
    code = code_of(largest)
    scale = scale_of(code)
    for place, v in zip(places, values):
        rows = v.shape[0]
        ref[place : place + rows, :] = jnp.round(v * tall(scale, rows)).astype(jnp.int32).astype(I16)
    ref[code_at : code_at + 16, :] = code.astype(jnp.int32).astype(I16)


def scales(codes):
    return scale_of(-codes.astype(F32))


def greet(devices):
    barrier = pltpu.get_barrier_semaphore()
    for device in devices:
        pl.semaphore_signal(barrier, inc=1, device_id=device, device_id_type=MESH)


def remote(src, dst, send, recv, device):
    return pltpu.make_async_remote_copy(
        src_ref=src, dst_ref=dst, send_sem=send, recv_sem=recv, device_id=device, device_id_type=MESH
    )


def split(x):
    hi = x.astype(BF)
    return hi, (x - hi.astype(F32)).astype(BF)


def dot(a, b):
    return lax.dot_general(a, b, (((1,), (0,)), ((), ())), preferred_element_type=F32)


def left(table, x):
    (th, tl), (xh, xl) = table, split(x)
    return dot(th, xh) + (dot(th, xl) + dot(tl, xh))


def right(x, table):
    (th, tl), (xh, xl) = table, split(x)
    return dot(xh, th) + (dot(xl, th) + dot(xh, tl))


def kernel(
    obj_ref, probe_ref, own_pos, lend_pos, lend_live, own_amp, recv_amp, th_ref, tl_ref, perm_ref,
    stage, grad_ref,
    win, probe, th, tl, perm, amp, lent, amp_sorted, terms, pg, where, live_of,
    out1, in1, relay1, out2, in2, relay2, edge,
    from_core, half, spread, pieces, deep_all, gathered,
    local, send1, recv1, send2, recv2, asend, arecv,
):
    row, col = lax.axis_index("row"), lax.axis_index("col")
    x, zl, core = lax.div(col, 4), lax.rem(lax.div(col, 2), 2), lax.rem(col, 2)
    zh, y = lax.div(row, 4), lax.rem(row, 4)
    plane, deep = x * 4 + y, zh * 2 + zl

    def dev(dr, dc):
        return (lax.rem(row + (16 + dr), 16), lax.rem(col + (16 + dc), 16))

    twin = (row, col + 1 - 2 * core)
    flat = []
    for d in range(1, 16):
        tx, ty = lax.rem(x + d // 4, 4), lax.rem(y + d % 4, 4)
        fx, fy = lax.rem(x + 4 - d // 4, 4), lax.rem(y + 4 - d % 4, 4)
        flat.append(((zh * 4 + ty, tx * 4 + zl * 2 + core), tx * 4 + ty, fx * 4 + fy))
    high = []
    for d in range(1, 8):
        there = lax.rem(deep + d, 8)
        high.append((lax.div(there, 2) * 4 + y, x * 4 + lax.rem(there, 2) * 2 + core))

    partners = [dev(*d) for d in ((1, 0), (-1, 0), (0, 1), (0, -1), (4, 0), (-4, 0), (3, 0), (-3, 0))]
    partners += [twin] + [f[0] for f in flat] + high
    greet(partners)
    loads = []
    for p in range(2):
        for j in range(4):
            loads.append((obj_ref.at[p, :, pl.ds(j * H, H)], win.at[p, j + 1, pl.ds(H, TILE), :]))
    loads += [(probe_ref, probe), (own_amp, amp), (perm_ref, perm), (th_ref, th), (tl_ref, tl)]
    loads = [pltpu.make_async_copy(s, d, local.at[k]) for k, (s, d) in enumerate(loads)]
    for copy in loads:
        copy.start()

    for k in range(OWN):
        where[2 * k] = jnp.clip(own_pos[0, k] - row * TILE + H, 0, TILE)
        where[2 * k + 1] = jnp.clip(own_pos[1, k] - col * TILE + H, 0, TILE)
        live_of[k] = jnp.float32(1.0)
    for k in range(FRAMES - OWN):
        where[2 * (OWN + k)] = jnp.clip(lend_pos[k, 0] - row * TILE + H, 0, TILE)
        where[2 * (OWN + k) + 1] = jnp.clip(lend_pos[k, 1] - col * TILE + H, 0, TILE)
        live_of[OWN + k] = lend_live[k].astype(F32)

    for copy in loads[:8]:
        copy.wait()

    def of_win(i, j):
        return [win[p, j + 1, (i + 1) * H : (i + 2) * H, :] for p in range(2)]

    def put_half(ref, k, blocks, code_mid):
        base = at_in(k)[0]
        values = [v for b in blocks for v in b]
        if code_mid:
            places, code_at = [base, base + H, base + 272, base + 272 + H], base + 256
        else:
            places, code_at = [base, base + H, base + 256, base + 256 + H], base + 512
        encode(ref, places, values, code_at)

    def put_strip(ref, k, blocks):
        base = at_in(k)[0]
        values = [v for b in blocks for v in b]
        encode(ref, [base + H * t for t in range(8)], values, base + 8 * H)

    put_half(out1, 1, [of_win(3, 1), of_win(3, 2)], False)
    put_half(out1, 3, [of_win(0, 1), of_win(0, 2)], False)
    put_half(out1, 0, [of_win(3, 0), of_win(3, 3)], True)
    put_half(out1, 2, [of_win(0, 0), of_win(0, 3)], True)
    put_strip(out1, 4, [of_win(i, 0) for i in range(4)])
    put_strip(out1, 5, [of_win(i, 3) for i in range(4)])
    pl.semaphore_wait(pltpu.get_barrier_semaphore(), len(partners))

    class Exchange:
        def __init__(self, out, inn, relay, send, recv):
            def go(k, there, device):
                return remote(view(out, k), view(inn, there), send.at[k], recv.at[there], device)

            self.down = [go(0, 0, dev(1, 0)), go(1, 1, dev(1, 0))]
            self.up = [go(2, 2, dev(-1, 0)), go(3, 3, dev(-1, 0))]
            self.lefts = go(4, 5, dev(0, -1))
            self.rights = go(5, 4, dev(0, 1))
            self.relays = [
                remote(view(out, 1), relay.at[0], send.at[1], recv.at[10], dev(-3, 0)),
                remote(view(out, 3), relay.at[1], send.at[3], recv.at[11], dev(3, 0)),
            ]
            self.onward = [
                remote(relay.at[0], view(inn, 1), send.at[10], recv.at[1], dev(4, 0)),
                remote(relay.at[1], view(inn, 3), send.at[11], recv.at[3], dev(-4, 0)),
            ]

        def start_second_halves(self):
            for turn, direct, relayed in ((3, self.down[1], self.relays[0]), (0, self.up[1], self.relays[1])):
                pl.when(y == turn)(relayed.start)
                pl.when(y != turn)(direct.start)

        def pass_on(self):
            for turn, k in ((0, 0), (3, 1)):

                def onward(k=k):
                    self.relays[k].wait_recv()
                    self.onward[k].start()

                pl.when(y == turn)(onward)

        def finish_sends(self):
            for copy in self.down + self.up + [self.lefts, self.rights]:
                copy.wait_send()
            pl.when(y == 0)(self.onward[0].wait_send)
            pl.when(y == 3)(self.onward[1].wait_send)

    first = Exchange(out1, in1, relay1, send1, recv1)
    first.start_second_halves()
    first.down[0].start()
    first.up[0].start()
    first.lefts.start()
    first.rights.start()
    lends = [
        remote(recv_amp.at[0], lent.at[0], asend.at[46], arecv.at[46], dev(0, -1)),
        remote(recv_amp.at[1], lent.at[1], asend.at[47], arecv.at[47], dev(0, 1)),
    ]

    for copy in loads[8:]:
        copy.wait()
    pg[...] = jnp.zeros_like(pg)
    edges = jnp.zeros((H, H), F32)

    def clear(f, carry):
        for p in range(2):
            for k in range(3):
                terms[f, p, k, :H, :] = edges
                terms[f, p, k, H + FR :, :] = edges
        return carry

    lax.fori_loop(0, FRAMES, clear, 0)
    first.pass_on()
    power = sum(probe[m, q] ** 2 for m in range(2) for q in range(2))
    inverse = 1.0 / (jnp.full((1, H), jnp.max(power), F32) + 1e-6)

    def sort_own(f, carry):
        amp_sorted[f] = dot(dot(perm[0], amp[f]).astype(BF), perm[1]).astype(BF)
        return carry

    lax.fori_loop(0, OWN, sort_own, 0)

    def open_blocks(ref, k, spots, first_at, code_at):
        base = at_in(k)[0]
        scale = tall(scales(ref[base + code_at : base + code_at + 16, :]), H)
        out = []
        for spot, at in zip(spots, first_at):
            out.append((spot, [ref[base + at + p * H : base + at + (p + 1) * H, :].astype(F32) * scale for p in range(2)]))
        return out

    def fill(k, spots, first_at, code_at):
        for (i, j), planes in open_blocks(in1, k, spots, first_at, code_at):
            for p in range(2):
                win[p, j, i * H : (i + 1) * H, :] = planes[p]

    corners = [
        (0, 0, 7, -1, 0), (0, 256, 6, 1, 1), (2, 0, 9, -1, 2), (2, 256, 8, 1, 3),
    ]
    forwards = []
    for k, at, there, side, n in corners:
        src = in1.at[pl.ds(at_in(k)[0] + at, CORNER)]
        forwards.append(remote(src, view(in1, there), send1.at[6 + n], recv1.at[there], dev(0, side)))
    first.down[0].wait_recv()
    forwards[0].start()
    forwards[1].start()
    first.up[0].wait_recv()
    forwards[2].start()
    forwards[3].start()
    fill(0, [(0, 1), (0, 4)], [0, 272], 256)
    fill(2, [(5, 1), (5, 4)], [0, 272], 256)
    first.rights.wait_recv()
    fill(4, [(i, 0) for i in range(1, 5)], [256 * t for t in range(4)], 1024)
    first.lefts.wait_recv()
    fill(5, [(i, 5) for i in range(1, 5)], [256 * t for t in range(4)], 1024)
    first.down[1].wait_recv()
    fill(1, [(0, 2), (0, 3)], [0, 256], 512)
    first.up[1].wait_recv()
    fill(3, [(5, 2), (5, 3)], [0, 256], 512)
    for n, (k, spot) in enumerate(((7, (0, 5)), (6, (0, 0)), (9, (5, 5)), (8, (5, 0)))):
        forwards[n].wait_recv()
        fill(k, [spot], [0 if n % 2 == 0 else 16], 256 if n % 2 == 0 else 0)
    for copy in lends:
        copy.start()
    lane = lax.broadcasted_iota(jnp.int32, (FR, H), 1)

    T = [(th[g], tl[g]) for g in range(2)]
    Tt = [(th[2 + g], tl[2 + g]) for g in range(2)]

    def two(ff, carry):
        S=[]; P={}; e={}; cols={}
        for u in range(2):
            f=2*ff+u
            r=where[2*f]; c=where[2*f+1]
            cb=lax.div(c,H); s=c-cb*H
            live=live_of[f]
            S.append((f,r,cb,s))
            for p in range(2):
                R=[pltpu.roll(win[p,jnp.minimum(cb+k,5),pl.ds(r,FR),:],lax.rem(H-s,H),axis=1) for k in range(3)]
                for h in range(2): P[u,p,h]=jnp.where(lane<H-s,R[h],R[h+1])*live
            for m in range(2):
                for h in range(2):
                    pr=probe[m,0,:,h*H:(h+1)*H]; pi=probe[m,1,:,h*H:(h+1)*H]
                    e[u,m,0,h]=pr*P[u,0,h]-pi*P[u,1,h]; e[u,m,1,h]=pr*P[u,1,h]+pi*P[u,0,h]
                for g in range(2):
                    a=[e[u,m,q,0]+e[u,m,q,1] if g==0 else e[u,m,q,0]-e[u,m,q,1] for q in range(2)]
                    cols[u,m,g]=right(jnp.concatenate(a,axis=1),Tt[g])
        far={}
        for u in range(2):
            for m in range(2):
                for g in range(2):
                    x=[]
                    for q in range(2):
                        whole=jnp.concatenate([cols[u,m,0][:,q*H:(q+1)*H],cols[u,m,1][:,q*H:(q+1)*H]],axis=1)
                        x.append(whole[:H]+whole[H:] if g==0 else whole[:H]-whole[H:])
                    far[u,m,g]=left(T[g],jnp.concatenate(x,axis=0))
        B={}
        for u in range(2):
            A=amp_sorted[S[u][0]].astype(F32)
            for g in range(2):
                power=sum(far[u,m,g][:H]**2+far[u,m,g][H:]**2 for m in range(2))
                keep=1.0-A[g*H:(g+1)*H]*lax.rsqrt(jnp.maximum(power,1.0))
                kk=jnp.concatenate([keep,keep],axis=0)
                for m in range(2):
                    B[u,m,g]=left(Tt[g],far[u,m,g]*kk)
        D={}
        for u in range(2):
            for m in range(2):
                z=[]
                for q in range(2):
                    a=B[u,m,0][q*H:(q+1)*H]; b=B[u,m,1][q*H:(q+1)*H]
                    z.append(jnp.concatenate([a+b,a-b],axis=0))
                for g in range(2):
                    D[u,m,g]=right(jnp.concatenate([z[0][:,g*H:(g+1)*H],z[1][:,g*H:(g+1)*H]],axis=1),T[g])
        o={}
        for u in range(2):
          for m in range(2):
            for h in range(2):
                br,bi=[ (D[u,m,0][:,q*H:(q+1)*H]+D[u,m,1][:,q*H:(q+1)*H]) if h==0 else (D[u,m,0][:,q*H:(q+1)*H]-D[u,m,1][:,q*H:(q+1)*H]) for q in range(2)]
                pr=probe[m,0,:,h*H:(h+1)*H]; pi=probe[m,1,:,h*H:(h+1)*H]
                x0=pr*br+pi*bi; x1=pr*bi-pi*br
                o[u,0,h]=x0 if m==0 else o[u,0,h]+x0
                o[u,1,h]=x1 if m==0 else o[u,1,h]+x1
                pg[pl.ds((m*2*2+h)*FR,FR),:]+=P[u,0,h]*br+P[u,1,h]*bi
                pg[pl.ds(((m*2+1)*2+h)*FR,FR),:]+=P[u,0,h]*bi-P[u,1,h]*br
        for u in range(2):
          f,r,cb,s=S[u]
          for p in range(2):
            R0=pltpu.roll(o[u,p,0],s,axis=1); R1=pltpu.roll(o[u,p,1],s,axis=1)
            low=lane<s
            blk=[jnp.where(low,0.0,R0),jnp.where(low,R0,R1),jnp.where(low,R1,0.0)]
            for k in range(3):
                terms[f,p,k,H:H+FR,:]=blk[k]
        return carry
    def each(f, carry):
        def lent_frames():
            for k in range(2):
                lends[k].wait_recv()
                amp_sorted[OWN + k] = dot(dot(perm[0], lent[k]).astype(BF), perm[1]).astype(BF)

        pl.when(f == OWN // 2)(lent_frames)
        return two(f, carry)

    lax.fori_loop(0, FRAMES // 2, each, 0)

    def at_rows(ref, index, rows):
        return ref.at[pl.ds(pl.multiple_of(index * rows, rows), rows)]

    swap = remote(at_rows(pg, 1 - core, 1024), from_core, asend.at[0], arecv.at[0], twin)
    swap.start()

    spots = [(where[2 * f], lax.div(where[2 * f + 1], H)) for f in range(FRAMES)]

    def block(i, j):
        planes = []
        for p in range(2):
            total = None
            for f, (r, cb) in enumerate(spots):
                k = j - cb
                at = jnp.where((k < 0) | (k > 2), 0, jnp.clip(i * H - r, -H, FR) + H)
                k = jnp.clip(k, 0, 2)
                part = terms[f, p, k, pl.ds(at, H), :]
                total = part if total is None else total + part
            planes.append(total * inverse)
        return planes

    second = Exchange(out2, in2, relay2, send2, recv2)
    base = OUT_ROWS
    aside = []
    for n, (j, side) in enumerate(((0, -1), (5, 1))):
        at = base + n * HALF
        encode(out2, [at, at + H, at + 256, at + 256 + H], block(0, j) + block(5, j), at + 512)
        there = base + (1 - n) * HALF
        aside.append(
            remote(out2.at[pl.ds(at, HALF)], in2.at[pl.ds(there, HALF)], send2.at[6 + n], recv2.at[7 - n], dev(0, side))
        )
        aside[-1].start()
    put_half(out2, 1, [block(5, 2), block(5, 3)], False)
    put_half(out2, 3, [block(0, 2), block(0, 3)], False)
    second.start_second_halves()

    swap.wait()
    half[...] = pg[pl.ds(pl.multiple_of(core * 1024, 1024), 1024), :] + from_core[...]
    def spread_out(k, carry):
        value = half[pl.ds(pl.multiple_of(k * 64, 64), 64), :]
        largest = jnp.abs(value[:16])
        for t in range(16, 64, 16):
            largest = jnp.maximum(largest, jnp.abs(value[t : t + 16]))
        code = code_of(largest)
        spread[k, :64, :] = jnp.round(value * tall(scale_of(code), 64)).astype(jnp.int32).astype(I16)
        spread[k, 64:, :] = code.astype(jnp.int32).astype(I16)
        return carry

    lax.fori_loop(0, 16, spread_out, 0)
    scatter = []
    for d, (device, there, _) in enumerate(flat):
        scatter.append(remote(spread.at[there], pieces.at[d], asend.at[1 + d], arecv.at[1 + d], device))
        scatter[-1].start()

    put_strip(out2, 4, [block(i, 0) for i in range(1, 5)])
    second.lefts.start()
    put_strip(out2, 5, [block(i, 5) for i in range(1, 5)])
    second.rights.start()
    for n, (i, j) in enumerate(((0, 1), (0, 4), (5, 1), (5, 4))):
        planes = block(i, j)
        for p in range(2):
            edge[n, p] = planes[p]
    second.pass_on()
    for n in range(2):
        aside[n].wait_recv()
    sums = {}
    for n, j in ((0, 1), (1, 4)):
        at = base + n * HALF
        scale = tall(scales(in2[at + 512 : at + 528, :]), H)
        for i, off, e in ((0, 0, n), (5, 256, 2 + n)):
            sums[(i, j)] = [edge[e, p] + in2[at + off + p * H : at + off + (p + 1) * H, :].astype(F32) * scale for p in range(2)]
    put_half(out2, 2, [sums[(0, 1)], sums[(0, 4)]], False)
    second.up[0].start()
    put_half(out2, 0, [sums[(5, 1)], sums[(5, 4)]], False)
    second.down[0].start()

    def piece_of(ref, k):
        return ref[k, :64, :].astype(F32) * tall(scales(ref[k, 64:, :]), 64)

    def put_piece(ref, k, value):
        largest = jnp.abs(value[:16])
        for t in range(16, 64, 16):
            largest = jnp.maximum(largest, jnp.abs(value[t : t + 16]))
        code = code_of(largest)
        ref[k, :64, :] = jnp.round(value * tall(scale_of(code), 64)).astype(jnp.int32).astype(I16)
        ref[k, 64:, :] = code.astype(jnp.int32).astype(I16)

    for copy in scatter:
        copy.wait()
    total = half[pl.ds(pl.multiple_of(plane * 64, 64), 64), :]
    for d in range(15):
        total = total + piece_of(pieces, d)
    put_piece(deep_all, deep, total)
    depth = []
    for d, device in enumerate(high):
        depth.append(remote(deep_all.at[deep], deep_all.at[deep], asend.at[16 + d], arecv.at[16 + d], device))
        depth[-1].start()

    for i in range(4):
        for j in range(4):
            planes = block(i + 1, j + 1)
            for p in range(2):
                stage[p, i * H : (i + 1) * H, j * H : (j + 1) * H] = win[p, j + 1, (i + 1) * H : (i + 2) * H, :] - planes[p]

    for copy in depth:
        copy.wait()
    total = piece_of(deep_all, 0)
    for k in range(1, 8):
        total = total + piece_of(deep_all, k)
    put_piece(gathered, core * 16 + plane, total * (1.0 / 1024.0))
    gather = []
    mine = gathered.at[core * 16 + plane]
    for d, (device, _, _) in enumerate(flat):
        gather.append(remote(mine, mine, asend.at[23 + d], arecv.at[23 + d], device))
        gather[-1].start()
    cross = [remote(mine, mine, asend.at[38], arecv.at[38], twin)]
    cross[0].start()

    def take(k, spots, first_at, code_at):
        for (i, j), planes in open_blocks(in2, k, spots, first_at, code_at):
            for p in range(2):
                spot = (p, slice(i * H, (i + 1) * H), slice(j * H, (j + 1) * H))
                stage[spot] = stage[spot] - planes[p]

    for d, (_, _, origin) in enumerate(flat):
        gather[d].wait_recv()
        part = gathered.at[core * 16 + origin]
        cross.append(remote(part, part, asend.at[48 + d], arecv.at[48 + d], twin))
        cross[-1].start()

    second.rights.wait_recv()
    take(4, [(i, 0) for i in range(4)], [256 * t for t in range(4)], 1024)
    second.lefts.wait_recv()
    take(5, [(i, 3) for i in range(4)], [256 * t for t in range(4)], 1024)

    second.down[1].wait_recv()
    take(1, [(0, 1), (0, 2)], [0, 256], 512)
    second.up[1].wait_recv()
    take(3, [(3, 1), (3, 2)], [0, 256], 512)
    second.down[0].wait_recv()
    take(0, [(0, 0), (0, 3)], [0, 256], 512)
    second.up[0].wait_recv()
    take(2, [(3, 0), (3, 3)], [0, 256], 512)

    def spell(k, carry):
        value = gathered[k, :64, :].astype(F32) * tall(scales(gathered[k, 64:, :]), 64)
        m, q, h, part = lax.div(k, 16), lax.rem(lax.div(k, 8), 2), lax.rem(lax.div(k, 4), 2), lax.rem(k, 4)
        grad_ref[m, q, pl.ds(pl.multiple_of(part * 64, 64), 64), pl.ds(pl.multiple_of(h * H, H), H)] = value
        return carry

    for copy in cross:
        copy.wait_recv()
    lax.fori_loop(0, 32, spell, 0)
    first.finish_sends()
    second.finish_sends()
    for copy in forwards + lends + aside + gather + cross:
        copy.wait_send()


def tables():
    n = np.arange(FR)
    angles = (n[:, None] * n[None, :] % FR) * (2.0 * math.pi / FR)
    cosine, sine = np.cos(angles) / 16.0, np.sin(angles) / 16.0
    both = []
    for g in range(2):
        c, s = cosine[g::2, :H], sine[g::2, :H]
        both.append(np.block([[c, s], [-s, c]]))
    both = np.stack(both + [b.T for b in both])
    hi = both.astype(np.float32).astype(ml_dtypes.bfloat16)
    lo = (both - hi.astype(np.float64)).astype(np.float32).astype(ml_dtypes.bfloat16)
    order = np.zeros((FR, FR), np.float32)
    order[np.arange(FR), np.concatenate([n[0::2], n[1::2]])] = 1.0
    return hi, lo, np.stack([order, order.T]).astype(ml_dtypes.bfloat16)


def shards(object_field, probe, own_pos, own_amp, lend_pos, lend_live, recv_amp):
    sm = pl.BlockSpec(memory_space=pltpu.SMEM)
    hbm = pl.BlockSpec(memory_space=pl.ANY)
    dma = pltpu.SemaphoreType.DMA
    hi, lo, order = tables()

    def vm(shape, dtype=F32):
        return pltpu.VMEM(shape, dtype)

    args = (object_field, probe, own_pos.T, lend_pos, lend_live, own_amp, recv_amp, jnp.asarray(hi), jnp.asarray(lo), jnp.asarray(order))
    held = [pltpu.with_memory_space_constraint(a, pltpu.HBM) for a in args]
    return pl.pallas_call(
        kernel,
        out_shape=(
            jax.ShapeDtypeStruct(object_field.shape, F32),
            jax.ShapeDtypeStruct(probe.shape, F32),
        ),
        in_specs=[hbm, hbm, sm, sm, sm, hbm, hbm, hbm, hbm, hbm],
        out_specs=(pl.BlockSpec(memory_space=pltpu.VMEM),) * 2,
        scratch_shapes=[
            vm((2, 6, WIN, H)),
            vm((2, 2, FR, FR)),
            vm((4, FR, FR), BF),
            vm((4, FR, FR), BF),
            vm((2, FR, FR), BF),
            vm((OWN, FR, FR), BF),
            vm((FRAMES - OWN, FR, FR), BF),
            vm((FRAMES, FR, FR), BF),
            vm((FRAMES, 2, 3, 2 * FR, H)),
            vm((2048, H)),
            pltpu.SMEM((2 * FRAMES,), jnp.int32),
            pltpu.SMEM((FRAMES,), F32),
            vm((OUT_ROWS, H), I16),
            vm((IN_ROWS, H), I16),
            vm((2, HALF, H), I16),
            vm((OUT_ROWS + 2 * HALF, H), I16),
            vm((OUT_ROWS + 2 * HALF, H), I16),
            vm((2, HALF, H), I16),
            vm((4, 2, H, H)),
            vm((1024, H)),
            vm((1024, H)),
            vm((16, PIECE, H), I16),
            vm((15, PIECE, H), I16),
            vm((8, PIECE, H), I16),
            vm((32, PIECE, H), I16),
            dma((13,)),
            dma((12,)),
            dma((12,)),
            dma((12,)),
            dma((12,)),
            dma((63,)),
            dma((63,)),
        ],
        compiler_params=pltpu.CompilerParams(collective_id=0, has_side_effects=True, vmem_limit_bytes=46 << 20),
        name="step",
    )(*held)


def solution(mesh):
    placed = (
        P(None, "row", "col"),
        P(),
        P(("row", "col"), None),
        P(("row", "col"), None, None),
        P(("row", "col"), None),
        P(("row", "col")),
        P(("row", "col"), None, None),
    )
    return jax.shard_map(
        shards, mesh=mesh, in_specs=placed, out_specs=(P(None, "row", "col"), P()), check_vma=False
    )
```

```python
import math

import jax
import jax.numpy as jnp
import ml_dtypes
import numpy as np
from jax import lax
from jax.experimental import pallas as pl
from jax.experimental.pallas import tpu as pltpu
from jax.sharding import PartitionSpec as P

MESH = pl.DeviceIdType.MESH
FR = 256
H = 128
TILE = 512
WIN = 768
OWN = 4
FRAMES = 6
F32 = jnp.float32
BF = jnp.bfloat16
I16 = jnp.int16

HALF = 4 * H + 16
STRIP = 8 * H + 16
BLOCK = 2 * H + 16
PIECE = 64 + 16


def at_in(k):
    if k < 8:
        return k * BLOCK, BLOCK
    if k < 10:
        return 8 * BLOCK + (k - 8) * STRIP, STRIP
    return 8 * BLOCK + 2 * STRIP + (k - 10) * BLOCK, BLOCK


COLUMNS = (0, 3, 1, 2)
ROUTES = {1: (-3, 4, 0), 2: (-1, 2, 2), 3: (-2, 3, 1)}


def view(ref, k):
    start, size = at_in(k)
    return ref.at[pl.ds(start, size)]


OUT_ROWS = 8 * BLOCK + 2 * STRIP
IN_ROWS = OUT_ROWS + 4 * BLOCK


def code_of(largest):
    octaves = jnp.log(jnp.maximum(largest, 1e-30)) * (1.0 / math.log(2.0))
    return jnp.floor(16.0 * (14.98 - octaves))


def scale_of(code):
    return jnp.exp(code * (math.log(2.0) / 16.0))


def tall(tile, rows):
    return jnp.concatenate([tile] * (rows // 16), axis=0)


def encode(ref, places, values, code_at):
    largest = None
    for v in values:
        for t in range(0, v.shape[0], 16):
            a = jnp.abs(v[t : t + 16])
            largest = a if largest is None else jnp.maximum(largest, a)
    code = code_of(largest)
    scale = scale_of(code)
    for place, v in zip(places, values):
        rows = v.shape[0]
        ref[place : place + rows, :] = jnp.round(v * tall(scale, rows)).astype(jnp.int32).astype(I16)
    ref[code_at : code_at + 16, :] = code.astype(jnp.int32).astype(I16)


def scales(codes):
    return scale_of(-codes.astype(F32))


def greet(devices):
    barrier = pltpu.get_barrier_semaphore()
    for device in devices:
        pl.semaphore_signal(barrier, inc=1, device_id=device, device_id_type=MESH)


def remote(src, dst, send, recv, device):
    return pltpu.make_async_remote_copy(
        src_ref=src, dst_ref=dst, send_sem=send, recv_sem=recv, device_id=device, device_id_type=MESH
    )


def split(x):
    hi = x.astype(BF)
    return hi, (x - hi.astype(F32)).astype(BF)


def dot(a, b):
    return lax.dot_general(a, b, (((1,), (0,)), ((), ())), preferred_element_type=F32)


def left(table, x):
    (th, tl), (xh, xl) = table, split(x)
    return dot(th, xh) + (dot(th, xl) + dot(tl, xh))


def right(x, table):
    (th, tl), (xh, xl) = table, split(x)
    return dot(xh, th) + (dot(xl, th) + dot(xh, tl))


def kernel(
    obj_ref, probe_ref, own_pos, lend_pos, lend_live, own_amp, recv_amp, th_ref, tl_ref, perm_ref,
    stage, grad_ref,
    win, probe, th, tl, perm, amp, lent, amp_sorted, terms, pg, where, live_of,
    out1, in1, relay1, out2, in2, relay2, edge,
    from_core, half, spread, pieces, deep_all, gathered,
    local, send1, recv1, send2, recv2, asend, arecv,
):
    row, col = lax.axis_index("row"), lax.axis_index("col")
    x, zl, core = lax.div(col, 4), lax.rem(lax.div(col, 2), 2), lax.rem(col, 2)
    zh, y = lax.div(row, 4), lax.rem(row, 4)
    plane, deep = x * 4 + y, zh * 2 + zl

    def dev(dr, dc):
        return (lax.rem(row + (16 + dr), 16), lax.rem(col + (16 + dc), 16))

    twin = (row, col + 1 - 2 * core)
    flat = []
    for d in range(1, 16):
        tx, ty = lax.rem(x + d // 4, 4), lax.rem(y + d % 4, 4)
        fx, fy = lax.rem(x + 4 - d // 4, 4), lax.rem(y + 4 - d % 4, 4)
        flat.append(((zh * 4 + ty, tx * 4 + zl * 2 + core), tx * 4 + ty, fx * 4 + fy))
    high = []
    for d in range(1, 8):
        there = lax.rem(deep + d, 8)
        high.append((lax.div(there, 2) * 4 + y, x * 4 + lax.rem(there, 2) * 2 + core))

    partners = [dev(*d) for d in ((1, 0), (-1, 0), (0, 1), (0, -1), (2, 0), (-2, 0), (3, 0), (-3, 0), (4, 0), (-4, 0))]
    partners += [twin] + [f[0] for f in flat] + high
    greet(partners)
    loads = []
    for p in range(2):
        for j in range(4):
            loads.append((obj_ref.at[p, :, pl.ds(j * H, H)], win.at[p, j + 1, pl.ds(H, TILE), :]))
    loads += [(probe_ref, probe), (own_amp, amp), (perm_ref, perm), (th_ref, th), (tl_ref, tl)]
    loads = [pltpu.make_async_copy(s, d, local.at[k]) for k, (s, d) in enumerate(loads)]
    for copy in loads:
        copy.start()

    for k in range(OWN):
        where[2 * k] = jnp.clip(own_pos[0, k] - row * TILE + H, 0, TILE)
        where[2 * k + 1] = jnp.clip(own_pos[1, k] - col * TILE + H, 0, TILE)
        live_of[k] = jnp.float32(1.0)
    for k in range(FRAMES - OWN):
        where[2 * (OWN + k)] = jnp.clip(lend_pos[k, 0] - row * TILE + H, 0, TILE)
        where[2 * (OWN + k) + 1] = jnp.clip(lend_pos[k, 1] - col * TILE + H, 0, TILE)
        live_of[OWN + k] = lend_live[k].astype(F32)

    for copy in loads[:8]:
        copy.wait()

    def of_win(i, j):
        return [win[p, j + 1, (i + 1) * H : (i + 2) * H, :] for p in range(2)]

    def put_block(ref, k, planes):
        base = at_in(k)[0]
        encode(ref, [base, base + H], planes, base + 2 * H)

    def put_strip(ref, k, blocks):
        base = at_in(k)[0]
        values = [v for b in blocks for v in b]
        encode(ref, [base + H * t for t in range(8)], values, base + 8 * H)

    for q in (3, 2, 1, 0):
        put_block(out1, q, of_win(3, COLUMNS[q]))
        put_block(out1, 4 + q, of_win(0, COLUMNS[q]))
    put_strip(out1, 8, [of_win(i, 0) for i in range(4)])
    put_strip(out1, 9, [of_win(i, 3) for i in range(4)])
    pl.semaphore_wait(pltpu.get_barrier_semaphore(), len(partners))

    class Exchange:
        def __init__(self, out, inn, relay, send, recv):
            def go(k, there, device):
                return remote(view(out, k), view(inn, there), send.at[k], recv.at[there], device)

            self.down = [go(q, q, dev(1, 0)) for q in range(4)]
            self.up = [go(4 + q, 4 + q, dev(-1, 0)) for q in range(4)]
            self.lefts = go(8, 9, dev(0, -1))
            self.rights = go(9, 8, dev(0, 1))
            self.routes = {}
            for q, (there, onward, at_y) in ROUTES.items():
                for way, sign, turn, k in ((0, 1, 3, q), (1, -1, 0, 4 + q)):
                    hop = remote(view(out, k), relay.at[way], send.at[k], recv.at[14 + way], dev(sign * there, 0))
                    rest = remote(relay.at[way], view(inn, k), send.at[14 + way], recv.at[k], dev(sign * onward, 0))
                    self.routes[q, way] = (turn, hop, at_y if way == 0 else 3 - at_y, rest)

        def start(self, q):
            for way, direct in ((0, self.down[q]), (1, self.up[q])):
                if q == 0:
                    direct.start()
                else:
                    turn, hop, _, _ = self.routes[q, way]
                    pl.when(y == turn)(hop.start)
                    pl.when(y != turn)(direct.start)

        def pass_on(self, q):
            for way in range(2):
                _, hop, at_y, rest = self.routes[q, way]

                def onward(hop=hop, rest=rest):
                    hop.wait_recv()
                    rest.start()

                pl.when(y == at_y)(onward)

        def finish_sends(self):
            for copy in self.down + self.up + [self.lefts, self.rights]:
                copy.wait_send()
            pl.when(y != 3)(self.routes[1, 0][3].wait_send)
            pl.when(y != 0)(self.routes[1, 1][3].wait_send)

    first = Exchange(out1, in1, relay1, send1, recv1)
    for q in (3, 2, 1, 0):
        first.start(q)
    first.lefts.start()
    first.rights.start()
    lends = [
        remote(recv_amp.at[0], lent.at[0], asend.at[46], arecv.at[46], dev(0, -1)),
        remote(recv_amp.at[1], lent.at[1], asend.at[47], arecv.at[47], dev(0, 1)),
    ]

    for copy in loads[8:]:
        copy.wait()
    pg[...] = jnp.zeros_like(pg)
    edges = jnp.zeros((H, H), F32)

    def clear(f, carry):
        for p in range(2):
            for k in range(3):
                terms[f, p, k, :H, :] = edges
                terms[f, p, k, H + FR :, :] = edges
        return carry

    lax.fori_loop(0, FRAMES, clear, 0)
    for q in (3, 2, 1):
        first.pass_on(q)
    power = sum(probe[m, q] ** 2 for m in range(2) for q in range(2))
    inverse = 1.0 / (jnp.full((1, H), jnp.max(power), F32) + 1e-6)

    def sort_own(f, carry):
        amp_sorted[f] = dot(dot(perm[0], amp[f]).astype(BF), perm[1]).astype(BF)
        return carry

    lax.fori_loop(0, OWN, sort_own, 0)

    def open_blocks(ref, k, spots):
        base, size = at_in(k)
        scale = tall(scales(ref[base + size - 16 : base + size, :]), H)
        out = []
        for n, spot in enumerate(spots):
            at = base + 2 * H * n
            out.append((spot, [ref[at + p * H : at + (p + 1) * H, :].astype(F32) * scale for p in range(2)]))
        return out

    def fill(k, spots):
        for (i, j), planes in open_blocks(in1, k, spots):
            for p in range(2):
                win[p, j, i * H : (i + 1) * H, :] = planes[p]

    forwards = []
    for n, (k, there, side) in enumerate(((0, 11, -1), (1, 10, 1), (4, 13, -1), (5, 12, 1))):
        forwards.append(remote(view(in1, k), view(in1, there), send1.at[10 + n], recv1.at[there], dev(0, side)))
    for n, copy in enumerate((first.down[0], first.down[1], first.up[0], first.up[1])):
        copy.wait_recv()
        forwards[n].start()
    for q in range(2):
        fill(q, [(0, 1 + COLUMNS[q])])
        fill(4 + q, [(5, 1 + COLUMNS[q])])
    first.rights.wait_recv()
    fill(8, [(i, 0) for i in range(1, 5)])
    first.lefts.wait_recv()
    fill(9, [(i, 5) for i in range(1, 5)])
    for q in (2, 3):
        first.down[q].wait_recv()
        fill(q, [(0, 1 + COLUMNS[q])])
        first.up[q].wait_recv()
        fill(4 + q, [(5, 1 + COLUMNS[q])])
    for n, (k, spot) in enumerate(((11, (0, 5)), (10, (0, 0)), (13, (5, 5)), (12, (5, 0)))):
        forwards[n].wait_recv()
        fill(k, [spot])
    for copy in lends:
        copy.start()
    lane = lax.broadcasted_iota(jnp.int32, (FR, H), 1)

    T = [(th[g], tl[g]) for g in range(2)]
    Tt = [(th[2 + g], tl[2 + g]) for g in range(2)]

    def two(ff, carry):
        S=[]; P={}; e={}; cols={}
        for u in range(2):
            f=2*ff+u
            r=where[2*f]; c=where[2*f+1]
            cb=lax.div(c,H); s=c-cb*H
            live=live_of[f]
            S.append((f,r,cb,s))
            for p in range(2):
                R=[pltpu.roll(win[p,jnp.minimum(cb+k,5),pl.ds(r,FR),:],lax.rem(H-s,H),axis=1) for k in range(3)]
                for h in range(2): P[u,p,h]=jnp.where(lane<H-s,R[h],R[h+1])*live
            for m in range(2):
                for h in range(2):
                    pr=probe[m,0,:,h*H:(h+1)*H]; pi=probe[m,1,:,h*H:(h+1)*H]
                    e[u,m,0,h]=pr*P[u,0,h]-pi*P[u,1,h]; e[u,m,1,h]=pr*P[u,1,h]+pi*P[u,0,h]
                for g in range(2):
                    a=[e[u,m,q,0]+e[u,m,q,1] if g==0 else e[u,m,q,0]-e[u,m,q,1] for q in range(2)]
                    cols[u,m,g]=right(jnp.concatenate(a,axis=1),Tt[g])
        far={}
        for u in range(2):
            for m in range(2):
                for g in range(2):
                    x=[]
                    for q in range(2):
                        whole=jnp.concatenate([cols[u,m,0][:,q*H:(q+1)*H],cols[u,m,1][:,q*H:(q+1)*H]],axis=1)
                        x.append(whole[:H]+whole[H:] if g==0 else whole[:H]-whole[H:])
                    far[u,m,g]=left(T[g],jnp.concatenate(x,axis=0))
        B={}
        for u in range(2):
            A=amp_sorted[S[u][0]].astype(F32)
            for g in range(2):
                power=sum(far[u,m,g][:H]**2+far[u,m,g][H:]**2 for m in range(2))
                keep=1.0-A[g*H:(g+1)*H]*lax.rsqrt(jnp.maximum(power,1.0))
                kk=jnp.concatenate([keep,keep],axis=0)
                for m in range(2):
                    B[u,m,g]=left(Tt[g],far[u,m,g]*kk)
        D={}
        for u in range(2):
            for m in range(2):
                z=[]
                for q in range(2):
                    a=B[u,m,0][q*H:(q+1)*H]; b=B[u,m,1][q*H:(q+1)*H]
                    z.append(jnp.concatenate([a+b,a-b],axis=0))
                for g in range(2):
                    D[u,m,g]=right(jnp.concatenate([z[0][:,g*H:(g+1)*H],z[1][:,g*H:(g+1)*H]],axis=1),T[g])
        o={}
        for u in range(2):
          for m in range(2):
            for h in range(2):
                br,bi=[ (D[u,m,0][:,q*H:(q+1)*H]+D[u,m,1][:,q*H:(q+1)*H]) if h==0 else (D[u,m,0][:,q*H:(q+1)*H]-D[u,m,1][:,q*H:(q+1)*H]) for q in range(2)]
                pr=probe[m,0,:,h*H:(h+1)*H]; pi=probe[m,1,:,h*H:(h+1)*H]
                x0=pr*br+pi*bi; x1=pr*bi-pi*br
                o[u,0,h]=x0 if m==0 else o[u,0,h]+x0
                o[u,1,h]=x1 if m==0 else o[u,1,h]+x1
                pg[pl.ds((m*2*2+h)*FR,FR),:]+=P[u,0,h]*br+P[u,1,h]*bi
                pg[pl.ds(((m*2+1)*2+h)*FR,FR),:]+=P[u,0,h]*bi-P[u,1,h]*br
        for u in range(2):
          f,r,cb,s=S[u]
          for p in range(2):
            R0=pltpu.roll(o[u,p,0],s,axis=1); R1=pltpu.roll(o[u,p,1],s,axis=1)
            low=lane<s
            blk=[jnp.where(low,0.0,R0),jnp.where(low,R0,R1),jnp.where(low,R1,0.0)]
            for k in range(3):
                terms[f,p,k,H:H+FR,:]=blk[k]
        return carry
    def each(f, carry):
        def lent_frames():
            for k in range(2):
                lends[k].wait_recv()
                amp_sorted[OWN + k] = dot(dot(perm[0], lent[k]).astype(BF), perm[1]).astype(BF)

        pl.when(f == OWN // 2)(lent_frames)
        return two(f, carry)

    lax.fori_loop(0, FRAMES // 2, each, 0)

    def at_rows(ref, index, rows):
        return ref.at[pl.ds(pl.multiple_of(index * rows, rows), rows)]

    swap = remote(at_rows(pg, 1 - core, 1024), from_core, asend.at[0], arecv.at[0], twin)
    swap.start()

    spots = [(where[2 * f], lax.div(where[2 * f + 1], H)) for f in range(FRAMES)]

    def block(i, j):
        planes = []
        for p in range(2):
            total = None
            for f, (r, cb) in enumerate(spots):
                k = j - cb
                at = jnp.where((k < 0) | (k > 2), 0, jnp.clip(i * H - r, -H, FR) + H)
                k = jnp.clip(k, 0, 2)
                part = terms[f, p, k, pl.ds(at, H), :]
                total = part if total is None else total + part
            planes.append(total * inverse)
        return planes

    second = Exchange(out2, in2, relay2, send2, recv2)
    base = OUT_ROWS
    aside = []
    for n, (j, side) in enumerate(((0, -1), (5, 1))):
        at = base + n * HALF
        encode(out2, [at, at + H, at + 256, at + 256 + H], block(0, j) + block(5, j), at + 512)
        there = base + (1 - n) * HALF
        aside.append(
            remote(out2.at[pl.ds(at, HALF)], in2.at[pl.ds(there, HALF)], send2.at[10 + n], recv2.at[11 - n], dev(0, side))
        )
        aside[-1].start()
    for q in (3, 2):
        put_block(out2, q, block(5, 1 + COLUMNS[q]))
        put_block(out2, 4 + q, block(0, 1 + COLUMNS[q]))
        second.start(q)

    swap.wait()
    half[...] = pg[pl.ds(pl.multiple_of(core * 1024, 1024), 1024), :] + from_core[...]
    def spread_out(k, carry):
        value = half[pl.ds(pl.multiple_of(k * 64, 64), 64), :]
        largest = jnp.abs(value[:16])
        for t in range(16, 64, 16):
            largest = jnp.maximum(largest, jnp.abs(value[t : t + 16]))
        code = code_of(largest)
        spread[k, :64, :] = jnp.round(value * tall(scale_of(code), 64)).astype(jnp.int32).astype(I16)
        spread[k, 64:, :] = code.astype(jnp.int32).astype(I16)
        return carry

    lax.fori_loop(0, 16, spread_out, 0)
    scatter = []
    for d, (device, there, _) in enumerate(flat):
        scatter.append(remote(spread.at[there], pieces.at[d], asend.at[1 + d], arecv.at[1 + d], device))
        scatter[-1].start()

    put_strip(out2, 8, [block(i, 0) for i in range(1, 5)])
    second.lefts.start()
    put_strip(out2, 9, [block(i, 5) for i in range(1, 5)])
    second.rights.start()
    for n, (i, j) in enumerate(((0, 1), (0, 4), (5, 1), (5, 4))):
        planes = block(i, j)
        for p in range(2):
            edge[n, p] = planes[p]
    second.pass_on(3)
    second.pass_on(2)
    for n in range(2):
        aside[n].wait_recv()
    sums = {}
    for n, j in ((0, 1), (1, 4)):
        at = base + n * HALF
        scale = tall(scales(in2[at + 512 : at + 528, :]), H)
        for i, off, e in ((0, 0, n), (5, 256, 2 + n)):
            sums[(i, j)] = [edge[e, p] + in2[at + off + p * H : at + off + (p + 1) * H, :].astype(F32) * scale for p in range(2)]
    for q in (1, 0):
        put_block(out2, q, sums[(5, 1 + COLUMNS[q])])
        put_block(out2, 4 + q, sums[(0, 1 + COLUMNS[q])])
        second.start(q)

    def piece_of(ref, k):
        return ref[k, :64, :].astype(F32) * tall(scales(ref[k, 64:, :]), 64)

    def put_piece(ref, k, value):
        largest = jnp.abs(value[:16])
        for t in range(16, 64, 16):
            largest = jnp.maximum(largest, jnp.abs(value[t : t + 16]))
        code = code_of(largest)
        ref[k, :64, :] = jnp.round(value * tall(scale_of(code), 64)).astype(jnp.int32).astype(I16)
        ref[k, 64:, :] = code.astype(jnp.int32).astype(I16)

    for copy in scatter:
        copy.wait()
    total = half[pl.ds(pl.multiple_of(plane * 64, 64), 64), :]
    for d in range(15):
        total = total + piece_of(pieces, d)
    put_piece(deep_all, deep, total)
    depth = []
    for d, device in enumerate(high):
        depth.append(remote(deep_all.at[deep], deep_all.at[deep], asend.at[16 + d], arecv.at[16 + d], device))
        depth[-1].start()

    for i in range(4):
        for j in range(4):
            planes = block(i + 1, j + 1)
            for p in range(2):
                stage[p, i * H : (i + 1) * H, j * H : (j + 1) * H] = win[p, j + 1, (i + 1) * H : (i + 2) * H, :] - planes[p]

    second.pass_on(1)
    for copy in depth:
        copy.wait()
    total = piece_of(deep_all, 0)
    for k in range(1, 8):
        total = total + piece_of(deep_all, k)
    put_piece(gathered, core * 16 + plane, total * (1.0 / 1024.0))
    gather = []
    mine = gathered.at[core * 16 + plane]
    for d, (device, _, _) in enumerate(flat):
        gather.append(remote(mine, mine, asend.at[23 + d], arecv.at[23 + d], device))
        gather[-1].start()
    cross = [remote(mine, mine, asend.at[38], arecv.at[38], twin)]
    cross[0].start()

    def take(k, spots):
        for (i, j), planes in open_blocks(in2, k, spots):
            for p in range(2):
                spot = (p, slice(i * H, (i + 1) * H), slice(j * H, (j + 1) * H))
                stage[spot] = stage[spot] - planes[p]

    for d, (_, _, origin) in enumerate(flat):
        gather[d].wait_recv()
        part = gathered.at[core * 16 + origin]
        cross.append(remote(part, part, asend.at[48 + d], arecv.at[48 + d], twin))
        cross[-1].start()

    second.rights.wait_recv()
    take(8, [(i, 0) for i in range(4)])
    second.lefts.wait_recv()
    take(9, [(i, 3) for i in range(4)])
    for q in (3, 2, 1, 0):
        second.down[q].wait_recv()
        take(q, [(0, COLUMNS[q])])
        second.up[q].wait_recv()
        take(4 + q, [(3, COLUMNS[q])])

    def spell(k, carry):
        value = gathered[k, :64, :].astype(F32) * tall(scales(gathered[k, 64:, :]), 64)
        m, q, h, part = lax.div(k, 16), lax.rem(lax.div(k, 8), 2), lax.rem(lax.div(k, 4), 2), lax.rem(k, 4)
        grad_ref[m, q, pl.ds(pl.multiple_of(part * 64, 64), 64), pl.ds(pl.multiple_of(h * H, H), H)] = value
        return carry

    for copy in cross:
        copy.wait_recv()
    lax.fori_loop(0, 32, spell, 0)
    first.finish_sends()
    second.finish_sends()
    for copy in forwards + lends + aside + gather + cross:
        copy.wait_send()


def tables():
    n = np.arange(FR)
    angles = (n[:, None] * n[None, :] % FR) * (2.0 * math.pi / FR)
    cosine, sine = np.cos(angles) / 16.0, np.sin(angles) / 16.0
    both = []
    for g in range(2):
        c, s = cosine[g::2, :H], sine[g::2, :H]
        both.append(np.block([[c, s], [-s, c]]))
    both = np.stack(both + [b.T for b in both])
    hi = both.astype(np.float32).astype(ml_dtypes.bfloat16)
    lo = (both - hi.astype(np.float64)).astype(np.float32).astype(ml_dtypes.bfloat16)
    order = np.zeros((FR, FR), np.float32)
    order[np.arange(FR), np.concatenate([n[0::2], n[1::2]])] = 1.0
    return hi, lo, np.stack([order, order.T]).astype(ml_dtypes.bfloat16)


def shards(object_field, probe, own_pos, own_amp, lend_pos, lend_live, recv_amp):
    sm = pl.BlockSpec(memory_space=pltpu.SMEM)
    hbm = pl.BlockSpec(memory_space=pl.ANY)
    dma = pltpu.SemaphoreType.DMA
    hi, lo, order = tables()

    def vm(shape, dtype=F32):
        return pltpu.VMEM(shape, dtype)

    args = (object_field, probe, own_pos.T, lend_pos, lend_live, own_amp, recv_amp, jnp.asarray(hi), jnp.asarray(lo), jnp.asarray(order))
    held = [pltpu.with_memory_space_constraint(a, pltpu.HBM) for a in args]
    return pl.pallas_call(
        kernel,
        out_shape=(
            jax.ShapeDtypeStruct(object_field.shape, F32),
            jax.ShapeDtypeStruct(probe.shape, F32),
        ),
        in_specs=[hbm, hbm, sm, sm, sm, hbm, hbm, hbm, hbm, hbm],
        out_specs=(pl.BlockSpec(memory_space=pltpu.VMEM),) * 2,
        scratch_shapes=[
            vm((2, 6, WIN, H)),
            vm((2, 2, FR, FR)),
            vm((4, FR, FR), BF),
            vm((4, FR, FR), BF),
            vm((2, FR, FR), BF),
            vm((OWN, FR, FR), BF),
            vm((FRAMES - OWN, FR, FR), BF),
            vm((FRAMES, FR, FR), BF),
            vm((FRAMES, 2, 3, 2 * FR, H)),
            vm((2048, H)),
            pltpu.SMEM((2 * FRAMES,), jnp.int32),
            pltpu.SMEM((FRAMES,), F32),
            vm((OUT_ROWS, H), I16),
            vm((IN_ROWS, H), I16),
            vm((2, BLOCK, H), I16),
            vm((OUT_ROWS + 2 * HALF, H), I16),
            vm((OUT_ROWS + 2 * HALF, H), I16),
            vm((2, BLOCK, H), I16),
            vm((4, 2, H, H)),
            vm((1024, H)),
            vm((1024, H)),
            vm((16, PIECE, H), I16),
            vm((15, PIECE, H), I16),
            vm((8, PIECE, H), I16),
            vm((32, PIECE, H), I16),
            dma((13,)),
            dma((16,)),
            dma((16,)),
            dma((16,)),
            dma((16,)),
            dma((63,)),
            dma((63,)),
        ],
        compiler_params=pltpu.CompilerParams(collective_id=0, has_side_effects=True, vmem_limit_bytes=46 << 20),
        name="step",
    )(*held)


def solution(mesh):
    placed = (
        P(None, "row", "col"),
        P(),
        P(("row", "col"), None),
        P(("row", "col"), None, None),
        P(("row", "col"), None),
        P(("row", "col")),
        P(("row", "col"), None, None),
    )
    return jax.shard_map(
        shards, mesh=mesh, in_specs=placed, out_specs=(P(None, "row", "col"), P()), check_vma=False
    )
```

```python
import math

import jax
import jax.numpy as jnp
import ml_dtypes
import numpy as np
from jax import lax
from jax.experimental import pallas as pl
from jax.experimental.pallas import tpu as pltpu
from jax.sharding import PartitionSpec as P

MESH = pl.DeviceIdType.MESH
FR = 256
H = 128
TILE = 512
WIN = 768
OWN = 4
FRAMES = 6
F32 = jnp.float32
BF = jnp.bfloat16
I16 = jnp.int16

HALF = 4 * H + 16
STRIP = 8 * H + 16
BLOCK = 2 * H + 16
PIECE = 64 + 16


def at_in(k):
    if k < 8:
        return k * BLOCK, BLOCK
    if k < 10:
        return 8 * BLOCK + (k - 8) * STRIP, STRIP
    return 8 * BLOCK + 2 * STRIP + (k - 10) * BLOCK, BLOCK


COLUMNS = (0, 3, 1, 2)
ROUTES = {1: (-3, 4, 0), 2: (-1, 2, 2), 3: (-2, 3, 1)}


def view(ref, k):
    start, size = at_in(k)
    return ref.at[pl.ds(start, size)]


OUT_ROWS = 8 * BLOCK + 2 * STRIP
IN_ROWS = OUT_ROWS + 4 * BLOCK


def code_of(largest):
    octaves = jnp.log(jnp.maximum(largest, 1e-30)) * (1.0 / math.log(2.0))
    return jnp.floor(16.0 * (14.98 - octaves))


def scale_of(code):
    return jnp.exp(code * (math.log(2.0) / 16.0))


def tall(tile, rows):
    return jnp.concatenate([tile] * (rows // 16), axis=0)


def encode(ref, places, values, code_at):
    largest = None
    for v in values:
        for t in range(0, v.shape[0], 16):
            a = jnp.abs(v[t : t + 16])
            largest = a if largest is None else jnp.maximum(largest, a)
    code = code_of(largest)
    scale = scale_of(code)
    for place, v in zip(places, values):
        rows = v.shape[0]
        ref[place : place + rows, :] = jnp.round(v * tall(scale, rows)).astype(jnp.int32).astype(I16)
    ref[code_at : code_at + 16, :] = code.astype(jnp.int32).astype(I16)


def scales(codes):
    return scale_of(-codes.astype(F32))


def remote(src, dst, send, recv, device):
    return pltpu.make_async_remote_copy(
        src_ref=src, dst_ref=dst, send_sem=send, recv_sem=recv, device_id=device, device_id_type=MESH
    )


def split(x):
    hi = x.astype(BF)
    return hi, (x - hi.astype(F32)).astype(BF)


def dot(a, b):
    return lax.dot_general(a, b, (((1,), (0,)), ((), ())), preferred_element_type=F32)


def left(table, x):
    (th, tl), (xh, xl) = table, split(x)
    return dot(th, xh) + (dot(th, xl) + dot(tl, xh))


def right(x, table):
    (th, tl), (xh, xl) = table, split(x)
    return dot(xh, th) + (dot(xl, th) + dot(xh, tl))


def kernel(
    obj_ref, probe_ref, own_pos, lend_pos, lend_live, own_amp, recv_amp, th_ref, tl_ref, perm_ref,
    stage, grad_ref,
    win, probe, th, tl, perm, amp, lent, amp_sorted, terms, pg, where, live_of,
    out1, in1, relay1, out2, in2, relay2, edge,
    from_core, half, spread, pieces, deep_all, gathered,
    local, send1, recv1, send2, recv2, asend, arecv,
):
    row, col = lax.axis_index("row"), lax.axis_index("col")
    x, zl, core = lax.div(col, 4), lax.rem(lax.div(col, 2), 2), lax.rem(col, 2)
    zh, y = lax.div(row, 4), lax.rem(row, 4)
    plane, deep = x * 4 + y, zh * 2 + zl

    def dev(dr, dc):
        return (lax.rem(row + (16 + dr), 16), lax.rem(col + (16 + dc), 16))

    twin = (row, col + 1 - 2 * core)
    flat = []
    for d in range(1, 16):
        tx, ty = lax.rem(x + d // 4, 4), lax.rem(y + d % 4, 4)
        fx, fy = lax.rem(x + 4 - d // 4, 4), lax.rem(y + 4 - d % 4, 4)
        flat.append(((zh * 4 + ty, tx * 4 + zl * 2 + core), tx * 4 + ty, fx * 4 + fy))
    high = []
    for d in range(1, 8):
        there = lax.rem(deep + d, 8)
        high.append((lax.div(there, 2) * 4 + y, x * 4 + lax.rem(there, 2) * 2 + core))

    loads = []
    for p in range(2):
        for j in range(4):
            loads.append((obj_ref.at[p, :, pl.ds(j * H, H)], win.at[p, j + 1, pl.ds(H, TILE), :]))
    loads += [(probe_ref, probe), (own_amp, amp), (perm_ref, perm), (th_ref, th), (tl_ref, tl)]
    loads = [pltpu.make_async_copy(s, d, local.at[k]) for k, (s, d) in enumerate(loads)]
    for copy in loads[:8]:
        copy.start()
    barrier = pltpu.get_barrier_semaphore()

    def hello(device):
        pl.semaphore_signal(barrier, inc=1, device_id=device, device_id_type=MESH)

    def first_row():
        for k in range(1, 5):
            hello(dev(-k, 0))

    def last_row():
        for k in range(1, 5):
            hello(dev(k, 0))

    pl.when(y == 0)(first_row)
    pl.when(y == 3)(last_row)
    partners = [dev(0, 1), dev(0, -1)] + [f[0] for f in flat] + high
    for device in partners:
        hello(device)
    for copy in loads[8:]:
        copy.start()

    for k in range(OWN):
        where[2 * k] = jnp.clip(own_pos[0, k] - row * TILE + H, 0, TILE)
        where[2 * k + 1] = jnp.clip(own_pos[1, k] - col * TILE + H, 0, TILE)
        live_of[k] = jnp.float32(1.0)
    for k in range(FRAMES - OWN):
        where[2 * (OWN + k)] = jnp.clip(lend_pos[k, 0] - row * TILE + H, 0, TILE)
        where[2 * (OWN + k) + 1] = jnp.clip(lend_pos[k, 1] - col * TILE + H, 0, TILE)
        live_of[OWN + k] = lend_live[k].astype(F32)

    for copy in loads[:8]:
        copy.wait()

    def of_win(i, j):
        return [win[p, j + 1, (i + 1) * H : (i + 2) * H, :] for p in range(2)]

    def put_block(ref, k, planes):
        base = at_in(k)[0]
        encode(ref, [base, base + H], planes, base + 2 * H)

    def put_strip(ref, k, blocks):
        base = at_in(k)[0]
        values = [v for b in blocks for v in b]
        encode(ref, [base + H * t for t in range(8)], values, base + 8 * H)

    for q in (3, 2, 1, 0):
        put_block(out1, q, of_win(3, COLUMNS[q]))
        put_block(out1, 4 + q, of_win(0, COLUMNS[q]))
    put_strip(out1, 8, [of_win(i, 0) for i in range(4)])
    put_strip(out1, 9, [of_win(i, 3) for i in range(4)])
    pl.semaphore_wait(barrier, len(partners) + 2)

    class Exchange:
        def __init__(self, out, inn, relay, send, recv):
            def go(k, there, device):
                return remote(view(out, k), view(inn, there), send.at[k], recv.at[there], device)

            self.down = [go(q, q, dev(1, 0)) for q in range(4)]
            self.up = [go(4 + q, 4 + q, dev(-1, 0)) for q in range(4)]
            self.lefts = go(8, 9, dev(0, -1))
            self.rights = go(9, 8, dev(0, 1))
            self.routes = {}
            for q, (there, onward, at_y) in ROUTES.items():
                for way, sign, turn, k in ((0, 1, 3, q), (1, -1, 0, 4 + q)):
                    hop = remote(view(out, k), relay.at[way], send.at[k], recv.at[14 + way], dev(sign * there, 0))
                    rest = remote(relay.at[way], view(inn, k), send.at[14 + way], recv.at[k], dev(sign * onward, 0))
                    self.routes[q, way] = (turn, hop, at_y if way == 0 else 3 - at_y, rest)

        def start(self, q):
            for way, direct in ((0, self.down[q]), (1, self.up[q])):
                if q == 0:
                    direct.start()
                else:
                    turn, hop, _, _ = self.routes[q, way]
                    pl.when(y == turn)(hop.start)
                    pl.when(y != turn)(direct.start)

        def pass_on(self, q):
            for way in range(2):
                _, hop, at_y, rest = self.routes[q, way]

                def onward(hop=hop, rest=rest):
                    hop.wait_recv()
                    rest.start()

                pl.when(y == at_y)(onward)

        def finish_sends(self):
            for copy in self.down + self.up + [self.lefts, self.rights]:
                copy.wait_send()
            pl.when(y != 3)(self.routes[1, 0][3].wait_send)
            pl.when(y != 0)(self.routes[1, 1][3].wait_send)

    first = Exchange(out1, in1, relay1, send1, recv1)
    for q in (3, 2, 1, 0):
        first.start(q)
    first.lefts.start()
    first.rights.start()
    lends = [
        remote(recv_amp.at[0], lent.at[0], asend.at[46], arecv.at[46], dev(0, -1)),
        remote(recv_amp.at[1], lent.at[1], asend.at[47], arecv.at[47], dev(0, 1)),
    ]

    for copy in loads[8:]:
        copy.wait()
    pg[...] = jnp.zeros_like(pg)
    edges = jnp.zeros((H, H), F32)

    def clear(f, carry):
        for p in range(2):
            for k in range(3):
                terms[f, p, k, :H, :] = edges
                terms[f, p, k, H + FR :, :] = edges
        return carry

    lax.fori_loop(0, FRAMES, clear, 0)
    for q in (3, 2, 1):
        first.pass_on(q)
    power = sum(probe[m, q] ** 2 for m in range(2) for q in range(2))
    inverse = 1.0 / (jnp.full((1, H), jnp.max(power), F32) + 1e-6)

    def sort_own(f, carry):
        amp_sorted[f] = dot(dot(perm[0], amp[f]).astype(BF), perm[1]).astype(BF)
        return carry

    lax.fori_loop(0, OWN, sort_own, 0)

    def open_blocks(ref, k, spots):
        base, size = at_in(k)
        scale = tall(scales(ref[base + size - 16 : base + size, :]), H)
        out = []
        for n, spot in enumerate(spots):
            at = base + 2 * H * n
            out.append((spot, [ref[at + p * H : at + (p + 1) * H, :].astype(F32) * scale for p in range(2)]))
        return out

    def fill(k, spots):
        for (i, j), planes in open_blocks(in1, k, spots):
            for p in range(2):
                win[p, j, i * H : (i + 1) * H, :] = planes[p]

    forwards = []
    for n, (k, there, side) in enumerate(((0, 11, -1), (1, 10, 1), (4, 13, -1), (5, 12, 1))):
        forwards.append(remote(view(in1, k), view(in1, there), send1.at[10 + n], recv1.at[there], dev(0, side)))
    for n, copy in enumerate((first.down[0], first.down[1], first.up[0], first.up[1])):
        copy.wait_recv()
        forwards[n].start()
    for q in range(2):
        fill(q, [(0, 1 + COLUMNS[q])])
        fill(4 + q, [(5, 1 + COLUMNS[q])])
    first.rights.wait_recv()
    fill(8, [(i, 0) for i in range(1, 5)])
    first.lefts.wait_recv()
    fill(9, [(i, 5) for i in range(1, 5)])
    for q in (2, 3):
        first.down[q].wait_recv()
        fill(q, [(0, 1 + COLUMNS[q])])
        first.up[q].wait_recv()
        fill(4 + q, [(5, 1 + COLUMNS[q])])
    for n, (k, spot) in enumerate(((11, (0, 5)), (10, (0, 0)), (13, (5, 5)), (12, (5, 0)))):
        forwards[n].wait_recv()
        fill(k, [spot])
    for copy in lends:
        copy.start()
    lane = lax.broadcasted_iota(jnp.int32, (FR, H), 1)

    T = [(th[g], tl[g]) for g in range(2)]
    Tt = [(th[2 + g], tl[2 + g]) for g in range(2)]

    def two(ff, carry):
        S=[]; P={}; e={}; cols={}
        for u in range(2):
            f=2*ff+u
            r=where[2*f]; c=where[2*f+1]
            cb=lax.div(c,H); s=c-cb*H
            live=live_of[f]
            S.append((f,r,cb,s))
            for p in range(2):
                R=[pltpu.roll(win[p,jnp.minimum(cb+k,5),pl.ds(r,FR),:],lax.rem(H-s,H),axis=1) for k in range(3)]
                for h in range(2): P[u,p,h]=jnp.where(lane<H-s,R[h],R[h+1])*live
            for m in range(2):
                for h in range(2):
                    pr=probe[m,0,:,h*H:(h+1)*H]; pi=probe[m,1,:,h*H:(h+1)*H]
                    e[u,m,0,h]=pr*P[u,0,h]-pi*P[u,1,h]; e[u,m,1,h]=pr*P[u,1,h]+pi*P[u,0,h]
                for g in range(2):
                    a=[e[u,m,q,0]+e[u,m,q,1] if g==0 else e[u,m,q,0]-e[u,m,q,1] for q in range(2)]
                    cols[u,m,g]=right(jnp.concatenate(a,axis=1),Tt[g])
        far={}
        for u in range(2):
            for m in range(2):
                for g in range(2):
                    x=[]
                    for q in range(2):
                        whole=jnp.concatenate([cols[u,m,0][:,q*H:(q+1)*H],cols[u,m,1][:,q*H:(q+1)*H]],axis=1)
                        x.append(whole[:H]+whole[H:] if g==0 else whole[:H]-whole[H:])
                    far[u,m,g]=left(T[g],jnp.concatenate(x,axis=0))
        B={}
        for u in range(2):
            A=amp_sorted[S[u][0]].astype(F32)
            for g in range(2):
                power=sum(far[u,m,g][:H]**2+far[u,m,g][H:]**2 for m in range(2))
                keep=1.0-A[g*H:(g+1)*H]*lax.rsqrt(jnp.maximum(power,1.0))
                kk=jnp.concatenate([keep,keep],axis=0)
                for m in range(2):
                    B[u,m,g]=left(Tt[g],far[u,m,g]*kk)
        D={}
        for u in range(2):
            for m in range(2):
                z=[]
                for q in range(2):
                    a=B[u,m,0][q*H:(q+1)*H]; b=B[u,m,1][q*H:(q+1)*H]
                    z.append(jnp.concatenate([a+b,a-b],axis=0))
                for g in range(2):
                    D[u,m,g]=right(jnp.concatenate([z[0][:,g*H:(g+1)*H],z[1][:,g*H:(g+1)*H]],axis=1),T[g])
        o={}
        for u in range(2):
          for m in range(2):
            for h in range(2):
                br,bi=[ (D[u,m,0][:,q*H:(q+1)*H]+D[u,m,1][:,q*H:(q+1)*H]) if h==0 else (D[u,m,0][:,q*H:(q+1)*H]-D[u,m,1][:,q*H:(q+1)*H]) for q in range(2)]
                pr=probe[m,0,:,h*H:(h+1)*H]; pi=probe[m,1,:,h*H:(h+1)*H]
                x0=pr*br+pi*bi; x1=pr*bi-pi*br
                o[u,0,h]=x0 if m==0 else o[u,0,h]+x0
                o[u,1,h]=x1 if m==0 else o[u,1,h]+x1
                pg[pl.ds((m*2*2+h)*FR,FR),:]+=P[u,0,h]*br+P[u,1,h]*bi
                pg[pl.ds(((m*2+1)*2+h)*FR,FR),:]+=P[u,0,h]*bi-P[u,1,h]*br
        for u in range(2):
          f,r,cb,s=S[u]
          for p in range(2):
            R0=pltpu.roll(o[u,p,0],s,axis=1); R1=pltpu.roll(o[u,p,1],s,axis=1)
            low=lane<s
            blk=[jnp.where(low,0.0,R0),jnp.where(low,R0,R1),jnp.where(low,R1,0.0)]
            for k in range(3):
                terms[f,p,k,H:H+FR,:]=blk[k]
        return carry
    def each(f, carry):
        def lent_frames():
            for k in range(2):
                lends[k].wait_recv()
                amp_sorted[OWN + k] = dot(dot(perm[0], lent[k]).astype(BF), perm[1]).astype(BF)

        pl.when(f == OWN // 2)(lent_frames)
        return two(f, carry)

    lax.fori_loop(0, FRAMES // 2, each, 0)

    swaps = []
    for c, dx in enumerate((2, 1, 3, 0)):
        rows = lax.rem(x + dx, 4) * 256
        there = pg.at[pl.ds(pl.multiple_of((1 - core) * 1024 + rows, 256), 256)]
        here = from_core.at[pl.ds(pl.multiple_of(rows, 256), 256)]
        k = 0 if c == 0 else 62 + c
        swaps.append(remote(there, here, asend.at[k], arecv.at[k], twin))
        swaps[-1].start()

    spots = [(where[2 * f], lax.div(where[2 * f + 1], H)) for f in range(FRAMES)]

    def block(i, j):
        planes = []
        for p in range(2):
            total = None
            for f, (r, cb) in enumerate(spots):
                k = j - cb
                at = jnp.where((k < 0) | (k > 2), 0, jnp.clip(i * H - r, -H, FR) + H)
                k = jnp.clip(k, 0, 2)
                part = terms[f, p, k, pl.ds(at, H), :]
                total = part if total is None else total + part
            planes.append(total * inverse)
        return planes

    second = Exchange(out2, in2, relay2, send2, recv2)
    base = OUT_ROWS
    aside = []
    for n, (j, side) in enumerate(((0, -1), (5, 1))):
        at = base + n * HALF
        encode(out2, [at, at + H, at + 256, at + 256 + H], block(0, j) + block(5, j), at + 512)
        there = base + (1 - n) * HALF
        aside.append(
            remote(out2.at[pl.ds(at, HALF)], in2.at[pl.ds(there, HALF)], send2.at[10 + n], recv2.at[11 - n], dev(0, side))
        )
        aside[-1].start()
    for q in (3, 2):
        put_block(out2, q, block(5, 1 + COLUMNS[q]))
        put_block(out2, 4 + q, block(0, 1 + COLUMNS[q]))
        second.start(q)

    def piece_of(ref, k):
        return ref[k, :64, :].astype(F32) * tall(scales(ref[k, 64:, :]), 64)

    def put_piece(ref, k, value):
        largest = jnp.abs(value[:16])
        for t in range(16, 64, 16):
            largest = jnp.maximum(largest, jnp.abs(value[t : t + 16]))
        code = code_of(largest)
        ref[k, :64, :] = jnp.round(value * tall(scale_of(code), 64)).astype(jnp.int32).astype(I16)
        ref[k, 64:, :] = code.astype(jnp.int32).astype(I16)

    scatter = []
    for c, dx in enumerate((2, 1, 3, 0)):
        swaps[c].wait_recv()
        for dy in (2, 1, 3, 0):
            k = lax.rem(x + dx, 4) * 4 + lax.rem(y + dy, 4)
            rows = k * 64
            value = pg[pl.ds(pl.multiple_of(core * 1024 + rows, 64), 64), :] + from_core[pl.ds(pl.multiple_of(rows, 64), 64), :]
            d = dx * 4 + dy - 1
            if d < 0:
                half[...] = value
                continue
            put_piece(spread, d, value)
            scatter.append(remote(spread.at[d], pieces.at[d], asend.at[1 + d], arecv.at[1 + d], flat[d][0]))
            scatter[-1].start()

    put_strip(out2, 8, [block(i, 0) for i in range(1, 5)])
    second.lefts.start()
    put_strip(out2, 9, [block(i, 5) for i in range(1, 5)])
    second.rights.start()
    for n, (i, j) in enumerate(((0, 1), (0, 4), (5, 1), (5, 4))):
        planes = block(i, j)
        for p in range(2):
            edge[n, p] = planes[p]
    second.pass_on(3)
    second.pass_on(2)
    for n in range(2):
        aside[n].wait_recv()
    sums = {}
    for n, j in ((0, 1), (1, 4)):
        at = base + n * HALF
        scale = tall(scales(in2[at + 512 : at + 528, :]), H)
        for i, off, e in ((0, 0, n), (5, 256, 2 + n)):
            sums[(i, j)] = [edge[e, p] + in2[at + off + p * H : at + off + (p + 1) * H, :].astype(F32) * scale for p in range(2)]
    for q in (1, 0):
        put_block(out2, q, sums[(5, 1 + COLUMNS[q])])
        put_block(out2, 4 + q, sums[(0, 1 + COLUMNS[q])])
        second.start(q)

    for copy in scatter:
        copy.wait()
    total = half[...]
    for d in range(15):
        total = total + piece_of(pieces, d)
    put_piece(deep_all, deep, total)
    depth = []
    for d in (3, 2, 4, 1, 5, 0, 6):
        device = high[d]
        depth.append(remote(deep_all.at[deep], deep_all.at[deep], asend.at[16 + d], arecv.at[16 + d], device))
        depth[-1].start()

    for i in range(4):
        for j in range(4):
            planes = block(i + 1, j + 1)
            for p in range(2):
                stage[p, i * H : (i + 1) * H, j * H : (j + 1) * H] = win[p, j + 1, (i + 1) * H : (i + 2) * H, :] - planes[p]

    second.pass_on(1)
    for copy in depth:
        copy.wait()
    total = piece_of(deep_all, 0)
    for k in range(1, 8):
        total = total + piece_of(deep_all, k)
    put_piece(gathered, core * 16 + plane, total * (1.0 / 1024.0))
    gather = []
    mine = gathered.at[core * 16 + plane]
    by_hops = sorted(range(15), key=lambda d: -((0, 1, 2, 1)[(d + 1) // 4] + (0, 1, 2, 1)[(d + 1) % 4]))
    for d, (device, _, _) in enumerate(flat):
        gather.append(remote(mine, mine, asend.at[23 + d], arecv.at[23 + d], device))
    for d in by_hops:
        gather[d].start()
    cross = [remote(mine, mine, asend.at[38], arecv.at[38], twin)]
    cross[0].start()

    def take(k, spots):
        for (i, j), planes in open_blocks(in2, k, spots):
            for p in range(2):
                spot = (p, slice(i * H, (i + 1) * H), slice(j * H, (j + 1) * H))
                stage[spot] = stage[spot] - planes[p]

    for d in reversed(by_hops):
        gather[d].wait_recv()
        part = gathered.at[core * 16 + flat[d][2]]
        cross.append(remote(part, part, asend.at[48 + d], arecv.at[48 + d], twin))
        cross[-1].start()

    second.rights.wait_recv()
    take(8, [(i, 0) for i in range(4)])
    second.lefts.wait_recv()
    take(9, [(i, 3) for i in range(4)])
    for q in (3, 2, 1, 0):
        second.down[q].wait_recv()
        take(q, [(0, COLUMNS[q])])
        second.up[q].wait_recv()
        take(4 + q, [(3, COLUMNS[q])])

    def spell(own):
        for k in range(16):
            value = piece_of(gathered, own * 16 + k)
            q, h, part = k // 8, k // 4 % 2, k % 4
            grad_ref[own, q, part * 64 : part * 64 + 64, h * H : (h + 1) * H] = value

    spell(core)
    for copy in cross:
        copy.wait_recv()
    spell(1 - core)
    for copy in swaps:
        copy.wait_send()
    first.finish_sends()
    second.finish_sends()
    for copy in forwards + lends + aside + gather + cross:
        copy.wait_send()


def write_out(obj_ref, grad_ref, new_ref, out_ref, sems):
    copies = []
    for p in range(2):
        for k in range(2):
            rows = pl.ds(k * 256, 256)
            copies.append((obj_ref.at[p, rows], new_ref.at[p, rows]))
    for m in range(2):
        for q in range(2):
            copies.append((grad_ref.at[m, q], out_ref.at[m, q]))
    copies = [pltpu.make_async_copy(a, b, sems.at[k]) for k, (a, b) in enumerate(copies)]
    for copy in copies:
        copy.start()
    for copy in copies:
        copy.wait()


def tables():
    n = np.arange(FR)
    angles = (n[:, None] * n[None, :] % FR) * (2.0 * math.pi / FR)
    cosine, sine = np.cos(angles) / 16.0, np.sin(angles) / 16.0
    both = []
    for g in range(2):
        c, s = cosine[g::2, :H], sine[g::2, :H]
        both.append(np.block([[c, s], [-s, c]]))
    both = np.stack(both + [b.T for b in both])
    hi = both.astype(np.float32).astype(ml_dtypes.bfloat16)
    lo = (both - hi.astype(np.float64)).astype(np.float32).astype(ml_dtypes.bfloat16)
    order = np.zeros((FR, FR), np.float32)
    order[np.arange(FR), np.concatenate([n[0::2], n[1::2]])] = 1.0
    return hi, lo, np.stack([order, order.T]).astype(ml_dtypes.bfloat16)


def shards(object_field, probe, own_pos, own_amp, lend_pos, lend_live, recv_amp):
    sm = pl.BlockSpec(memory_space=pltpu.SMEM)
    hbm = pl.BlockSpec(memory_space=pl.ANY)
    dma = pltpu.SemaphoreType.DMA
    hi, lo, order = tables()

    def vm(shape, dtype=F32):
        return pltpu.VMEM(shape, dtype)

    args = (object_field, probe, own_pos.T, lend_pos, lend_live, own_amp, recv_amp, jnp.asarray(hi), jnp.asarray(lo), jnp.asarray(order))
    held = [pltpu.with_memory_space_constraint(a, pltpu.HBM) for a in args]
    new_object, probe_grad = pl.pallas_call(
        kernel,
        out_shape=(
            jax.ShapeDtypeStruct(object_field.shape, F32),
            jax.ShapeDtypeStruct(probe.shape, F32),
        ),
        in_specs=[hbm, hbm, sm, sm, sm, hbm, hbm, hbm, hbm, hbm],
        out_specs=(pl.BlockSpec(memory_space=pltpu.VMEM),) * 2,
        scratch_shapes=[
            vm((2, 6, WIN, H)),
            vm((2, 2, FR, FR)),
            vm((4, FR, FR), BF),
            vm((4, FR, FR), BF),
            vm((2, FR, FR), BF),
            vm((OWN, FR, FR), BF),
            vm((FRAMES - OWN, FR, FR), BF),
            vm((FRAMES, FR, FR), BF),
            vm((FRAMES, 2, 3, 2 * FR, H)),
            vm((2048, H)),
            pltpu.SMEM((2 * FRAMES,), jnp.int32),
            pltpu.SMEM((FRAMES,), F32),
            vm((OUT_ROWS, H), I16),
            vm((IN_ROWS, H), I16),
            vm((2, BLOCK, H), I16),
            vm((OUT_ROWS + 2 * HALF, H), I16),
            vm((OUT_ROWS + 2 * HALF, H), I16),
            vm((2, BLOCK, H), I16),
            vm((4, 2, H, H)),
            vm((1024, H)),
            vm((64, H)),
            vm((15, PIECE, H), I16),
            vm((15, PIECE, H), I16),
            vm((8, PIECE, H), I16),
            vm((32, PIECE, H), I16),
            dma((13,)),
            dma((16,)),
            dma((16,)),
            dma((16,)),
            dma((16,)),
            dma((66,)),
            dma((66,)),
        ],
        compiler_params=pltpu.CompilerParams(collective_id=0, has_side_effects=True, vmem_limit_bytes=46 << 20),
        name="step",
    )(*held)
    return pl.pallas_call(
        write_out,
        out_shape=(
            jax.ShapeDtypeStruct(object_field.shape, F32),
            jax.ShapeDtypeStruct(probe.shape, F32),
        ),
        in_specs=[pl.BlockSpec(memory_space=pltpu.VMEM)] * 2,
        out_specs=(hbm, hbm),
        scratch_shapes=[dma((8,))],
        compiler_params=pltpu.CompilerParams(vmem_limit_bytes=8 << 20),
        name="write_out",
    )(new_object, probe_grad)


def solution(mesh):
    placed = (
        P(None, "row", "col"),
        P(),
        P(("row", "col"), None),
        P(("row", "col"), None, None),
        P(("row", "col"), None),
        P(("row", "col")),
        P(("row", "col"), None, None),
    )
    return jax.shard_map(
        shards, mesh=mesh, in_specs=placed, out_specs=(P(None, "row", "col"), P()), check_vma=False
    )
```

```python
import math

import jax
import jax.numpy as jnp
import ml_dtypes
import numpy as np
from jax import lax
from jax.experimental import pallas as pl
from jax.experimental.pallas import tpu as pltpu
from jax.sharding import PartitionSpec as P

MESH = pl.DeviceIdType.MESH
FR = 256
H = 128
TILE = 512
WIN = 768
OWN = 4
FRAMES = 6
F32 = jnp.float32
BF = jnp.bfloat16
I16 = jnp.int16

HALF = 4 * H + 16
STRIP = 8 * H + 16
BLOCK = 2 * H + 16
PIECE = 64 + 16


def at_in(k):
    if k < 8:
        return k * BLOCK, BLOCK
    if k < 10:
        return 8 * BLOCK + (k - 8) * STRIP, STRIP
    return 8 * BLOCK + 2 * STRIP + (k - 10) * BLOCK, BLOCK


COLUMNS = (0, 3, 1, 2)
ROUTES = {1: (-3, 4, 0), 2: (-1, 2, 2), 3: (-2, 3, 1)}


def view(ref, k):
    start, size = at_in(k)
    return ref.at[pl.ds(start, size)]


OUT_ROWS = 8 * BLOCK + 2 * STRIP
IN_ROWS = OUT_ROWS + 4 * BLOCK


def code_of(largest):
    octaves = jnp.log(jnp.maximum(largest, 1e-30)) * (1.0 / math.log(2.0))
    return jnp.floor(16.0 * (14.98 - octaves))


def scale_of(code):
    return jnp.exp(code * (math.log(2.0) / 16.0))


def tall(tile, rows):
    return jnp.concatenate([tile] * (rows // 16), axis=0)


def encode(ref, places, values, code_at):
    largest = None
    for v in values:
        for t in range(0, v.shape[0], 16):
            a = jnp.abs(v[t : t + 16])
            largest = a if largest is None else jnp.maximum(largest, a)
    code = code_of(largest)
    scale = scale_of(code)
    for place, v in zip(places, values):
        rows = v.shape[0]
        ref[place : place + rows, :] = jnp.round(v * tall(scale, rows)).astype(jnp.int32).astype(I16)
    ref[code_at : code_at + 16, :] = code.astype(jnp.int32).astype(I16)


def scales(codes):
    return scale_of(-codes.astype(F32))


def remote(src, dst, send, recv, device):
    return pltpu.make_async_remote_copy(
        src_ref=src, dst_ref=dst, send_sem=send, recv_sem=recv, device_id=device, device_id_type=MESH
    )


def split(x):
    hi = x.astype(BF)
    return hi, (x - hi.astype(F32)).astype(BF)


def dot(a, b):
    return lax.dot_general(a, b, (((1,), (0,)), ((), ())), preferred_element_type=F32)


def turned_right(x, table):
    (th, tl), (xh, xl) = table, split(x)

    def turned(a, b):
        return lax.dot_general(a, b, (((0,), (0,)), ((), ())), preferred_element_type=F32)

    return turned(xh, th) + (turned(xl, th) + turned(xh, tl))


def right(x, table):
    (th, tl), (xh, xl) = table, split(x)
    return dot(xh, th) + (dot(xl, th) + dot(xh, tl))


def kernel(
    obj_ref, probe_ref, own_pos, lend_pos, lend_live, own_amp, recv_amp, th_ref, tl_ref, perm_ref,
    stage, grad_ref,
    win, probe, th, tl, perm, amp, lent, amp_sorted, terms, pg, where, live_of,
    out1, in1, relay1, out2, in2, relay2, edge,
    from_core, half, spread, pieces, deep_all, gathered,
    local, send1, recv1, send2, recv2, asend, arecv,
):
    row, col = lax.axis_index("row"), lax.axis_index("col")
    x, zl, core = lax.div(col, 4), lax.rem(lax.div(col, 2), 2), lax.rem(col, 2)
    zh, y = lax.div(row, 4), lax.rem(row, 4)
    plane, deep = x * 4 + y, zh * 2 + zl

    def dev(dr, dc):
        return (lax.rem(row + (16 + dr), 16), lax.rem(col + (16 + dc), 16))

    twin = (row, col + 1 - 2 * core)
    flat = []
    for d in range(1, 16):
        tx, ty = lax.rem(x + d // 4, 4), lax.rem(y + d % 4, 4)
        fx, fy = lax.rem(x + 4 - d // 4, 4), lax.rem(y + 4 - d % 4, 4)
        flat.append(((zh * 4 + ty, tx * 4 + zl * 2 + core), tx * 4 + ty, fx * 4 + fy))
    high = []
    for d in range(1, 8):
        there = lax.rem(deep + d, 8)
        high.append((lax.div(there, 2) * 4 + y, x * 4 + lax.rem(there, 2) * 2 + core))

    loads = []
    for p in range(2):
        for j in range(4):
            loads.append((obj_ref.at[p, :, pl.ds(j * H, H)], win.at[p, j + 1, pl.ds(H, TILE), :]))
    loads += [(probe_ref, probe), (own_amp, amp), (perm_ref, perm), (th_ref, th), (tl_ref, tl)]
    loads = [pltpu.make_async_copy(s, d, local.at[k]) for k, (s, d) in enumerate(loads)]
    for copy in loads[:8]:
        copy.start()
    barrier = pltpu.get_barrier_semaphore()

    def hello(device):
        pl.semaphore_signal(barrier, inc=1, device_id=device, device_id_type=MESH)

    def first_row():
        for k in range(1, 5):
            hello(dev(-k, 0))

    def last_row():
        for k in range(1, 5):
            hello(dev(k, 0))

    pl.when(y == 0)(first_row)
    pl.when(y == 3)(last_row)
    partners = [dev(0, 1), dev(0, -1)] + [f[0] for f in flat] + high
    for device in partners:
        hello(device)
    for copy in loads[8:]:
        copy.start()

    for k in range(OWN):
        where[2 * k] = jnp.clip(own_pos[0, k] - row * TILE + H, 0, TILE)
        where[2 * k + 1] = jnp.clip(own_pos[1, k] - col * TILE + H, 0, TILE)
        live_of[k] = jnp.float32(1.0)
    for k in range(FRAMES - OWN):
        where[2 * (OWN + k)] = jnp.clip(lend_pos[k, 0] - row * TILE + H, 0, TILE)
        where[2 * (OWN + k) + 1] = jnp.clip(lend_pos[k, 1] - col * TILE + H, 0, TILE)
        live_of[OWN + k] = lend_live[k].astype(F32)

    for copy in loads[:8]:
        copy.wait()

    def of_win(i, j):
        return [win[p, j + 1, (i + 1) * H : (i + 2) * H, :] for p in range(2)]

    def put_block(ref, k, planes):
        base = at_in(k)[0]
        encode(ref, [base, base + H], planes, base + 2 * H)

    def put_strip(ref, k, blocks):
        base = at_in(k)[0]
        values = [v for b in blocks for v in b]
        encode(ref, [base + H * t for t in range(8)], values, base + 8 * H)

    for q in (3, 2, 1, 0):
        put_block(out1, q, of_win(3, COLUMNS[q]))
        put_block(out1, 4 + q, of_win(0, COLUMNS[q]))
    put_strip(out1, 8, [of_win(i, 0) for i in range(4)])
    put_strip(out1, 9, [of_win(i, 3) for i in range(4)])
    pl.semaphore_wait(barrier, len(partners) + 2)

    class Exchange:
        def __init__(self, out, inn, relay, send, recv):
            def go(k, there, device):
                return remote(view(out, k), view(inn, there), send.at[k], recv.at[there], device)

            self.down = [go(q, q, dev(1, 0)) for q in range(4)]
            self.up = [go(4 + q, 4 + q, dev(-1, 0)) for q in range(4)]
            self.lefts = go(8, 9, dev(0, -1))
            self.rights = go(9, 8, dev(0, 1))
            self.routes = {}
            for q, (there, onward, at_y) in ROUTES.items():
                for way, sign, turn, k in ((0, 1, 3, q), (1, -1, 0, 4 + q)):
                    hop = remote(view(out, k), relay.at[way], send.at[k], recv.at[14 + way], dev(sign * there, 0))
                    rest = remote(relay.at[way], view(inn, k), send.at[14 + way], recv.at[k], dev(sign * onward, 0))
                    self.routes[q, way] = (turn, hop, at_y if way == 0 else 3 - at_y, rest)

        def start(self, q):
            for way, direct in ((0, self.down[q]), (1, self.up[q])):
                if q == 0:
                    direct.start()
                else:
                    turn, hop, _, _ = self.routes[q, way]
                    pl.when(y == turn)(hop.start)
                    pl.when(y != turn)(direct.start)

        def pass_on(self, q):
            for way in range(2):
                _, hop, at_y, rest = self.routes[q, way]

                def onward(hop=hop, rest=rest):
                    hop.wait_recv()
                    rest.start()

                pl.when(y == at_y)(onward)

        def finish_sends(self):
            for copy in self.down + self.up + [self.lefts, self.rights]:
                copy.wait_send()
            pl.when(y != 3)(self.routes[1, 0][3].wait_send)
            pl.when(y != 0)(self.routes[1, 1][3].wait_send)

    first = Exchange(out1, in1, relay1, send1, recv1)
    for q in (3, 2, 1, 0):
        first.start(q)
    first.lefts.start()
    first.rights.start()
    lends = [
        remote(recv_amp.at[0], lent.at[0], asend.at[46], arecv.at[46], dev(0, -1)),
        remote(recv_amp.at[1], lent.at[1], asend.at[47], arecv.at[47], dev(0, 1)),
    ]

    for copy in loads[8:]:
        copy.wait()
    pg[...] = jnp.zeros_like(pg)
    edges = jnp.zeros((H, H), F32)

    def clear(f, carry):
        for p in range(2):
            for k in range(3):
                terms[f, p, k, :H, :] = edges
                terms[f, p, k, H + FR :, :] = edges
        return carry

    lax.fori_loop(0, FRAMES, clear, 0)
    for q in (3, 2, 1):
        first.pass_on(q)
    power = sum(probe[m, q] ** 2 for m in range(2) for q in range(2))
    inverse = 1.0 / (jnp.full((1, H), jnp.max(power), F32) + 1e-6)

    def sort_own(f, carry):
        amp_sorted[f] = dot(dot(perm[0], amp[f]).astype(BF), perm[1]).T.astype(BF)
        return carry

    lax.fori_loop(0, OWN, sort_own, 0)

    def open_blocks(ref, k, spots):
        base, size = at_in(k)
        scale = tall(scales(ref[base + size - 16 : base + size, :]), H)
        out = []
        for n, spot in enumerate(spots):
            at = base + 2 * H * n
            out.append((spot, [ref[at + p * H : at + (p + 1) * H, :].astype(F32) * scale for p in range(2)]))
        return out

    def fill(k, spots):
        for (i, j), planes in open_blocks(in1, k, spots):
            for p in range(2):
                win[p, j, i * H : (i + 1) * H, :] = planes[p]

    forwards = []
    for n, (k, there, side) in enumerate(((0, 11, -1), (1, 10, 1), (4, 13, -1), (5, 12, 1))):
        forwards.append(remote(view(in1, k), view(in1, there), send1.at[10 + n], recv1.at[there], dev(0, side)))
    for n, copy in enumerate((first.down[0], first.down[1], first.up[0], first.up[1])):
        copy.wait_recv()
        forwards[n].start()
    for q in range(2):
        fill(q, [(0, 1 + COLUMNS[q])])
        fill(4 + q, [(5, 1 + COLUMNS[q])])
    first.rights.wait_recv()
    fill(8, [(i, 0) for i in range(1, 5)])
    first.lefts.wait_recv()
    fill(9, [(i, 5) for i in range(1, 5)])
    for q in (2, 3):
        first.down[q].wait_recv()
        fill(q, [(0, 1 + COLUMNS[q])])
        first.up[q].wait_recv()
        fill(4 + q, [(5, 1 + COLUMNS[q])])
    for n, (k, spot) in enumerate(((11, (0, 5)), (10, (0, 0)), (13, (5, 5)), (12, (5, 0)))):
        forwards[n].wait_recv()
        fill(k, [spot])
    for copy in lends:
        copy.start()
    lane = lax.broadcasted_iota(jnp.int32, (FR, H), 1)

    T = [(th[g], tl[g]) for g in range(2)]
    Tt = [(th[2 + g], tl[2 + g]) for g in range(2)]

    def two(ff, carry):
        S=[]; P={}; e={}; cols={}
        for u in range(2):
            f=2*ff+u
            r=where[2*f]; c=where[2*f+1]
            cb=lax.div(c,H); s=c-cb*H
            live=live_of[f]
            S.append((f,r,cb,s))
            for p in range(2):
                R=[pltpu.roll(win[p,jnp.minimum(cb+k,5),pl.ds(r,FR),:],lax.rem(H-s,H),axis=1) for k in range(3)]
                for h in range(2): P[u,p,h]=jnp.where(lane<H-s,R[h],R[h+1])*live
            for m in range(2):
                for h in range(2):
                    pr=probe[m,0,:,h*H:(h+1)*H]; pi=probe[m,1,:,h*H:(h+1)*H]
                    e[u,m,0,h]=pr*P[u,0,h]-pi*P[u,1,h]; e[u,m,1,h]=pr*P[u,1,h]+pi*P[u,0,h]
                for g in range(2):
                    a=[e[u,m,q,0]+e[u,m,q,1] if g==0 else e[u,m,q,0]-e[u,m,q,1] for q in range(2)]
                    cols[u,m,g]=right(jnp.concatenate(a,axis=1),Tt[g])
        far={}
        for u in range(2):
            for m in range(2):
                for g in range(2):
                    x=[]
                    for q in range(2):
                        whole=jnp.concatenate([cols[u,m,0][:,q*H:(q+1)*H],cols[u,m,1][:,q*H:(q+1)*H]],axis=1)
                        x.append(whole[:H]+whole[H:] if g==0 else whole[:H]-whole[H:])
                    far[u,m,g]=turned_right(jnp.concatenate(x,axis=0),Tt[g])
        B={}
        for u in range(2):
            A=amp_sorted[S[u][0]].astype(F32)
            for g in range(2):
                power=sum(far[u,m,g][:,:H]**2+far[u,m,g][:,H:]**2 for m in range(2))
                keep=1.0-A[:,g*H:(g+1)*H]*lax.rsqrt(jnp.maximum(power,1.0))
                kk=jnp.concatenate([keep,keep],axis=1)
                for m in range(2):
                    B[u,m,g]=right(far[u,m,g]*kk,T[g])
        D={}
        for u in range(2):
            for m in range(2):
                z=[]
                for q in range(2):
                    a=B[u,m,0][:,q*H:(q+1)*H]; b=B[u,m,1][:,q*H:(q+1)*H]
                    z.append(jnp.concatenate([a+b,a-b],axis=1))
                for g in range(2):
                    D[u,m,g]=turned_right(jnp.concatenate([z[0][g*H:(g+1)*H],z[1][g*H:(g+1)*H]],axis=0),T[g])
        o={}
        for u in range(2):
          for m in range(2):
            for h in range(2):
                br,bi=[ (D[u,m,0][:,q*H:(q+1)*H]+D[u,m,1][:,q*H:(q+1)*H]) if h==0 else (D[u,m,0][:,q*H:(q+1)*H]-D[u,m,1][:,q*H:(q+1)*H]) for q in range(2)]
                pr=probe[m,0,:,h*H:(h+1)*H]; pi=probe[m,1,:,h*H:(h+1)*H]
                x0=pr*br+pi*bi; x1=pr*bi-pi*br
                o[u,0,h]=x0 if m==0 else o[u,0,h]+x0
                o[u,1,h]=x1 if m==0 else o[u,1,h]+x1
                pg[pl.ds((m*2*2+h)*FR,FR),:]+=P[u,0,h]*br+P[u,1,h]*bi
                pg[pl.ds(((m*2+1)*2+h)*FR,FR),:]+=P[u,0,h]*bi-P[u,1,h]*br
        for u in range(2):
          f,r,cb,s=S[u]
          for p in range(2):
            R0=pltpu.roll(o[u,p,0],s,axis=1); R1=pltpu.roll(o[u,p,1],s,axis=1)
            low=lane<s
            blk=[jnp.where(low,0.0,R0),jnp.where(low,R0,R1),jnp.where(low,R1,0.0)]
            for k in range(3):
                terms[f,p,k,H:H+FR,:]=blk[k]
        return carry
    def each(f, carry):
        def lent_frames():
            for k in range(2):
                lends[k].wait_recv()
                amp_sorted[OWN + k] = dot(dot(perm[0], lent[k]).astype(BF), perm[1]).T.astype(BF)

        pl.when(f == OWN // 2)(lent_frames)
        return two(f, carry)

    lax.fori_loop(0, FRAMES // 2, each, 0)

    swaps = []
    for c, dx in enumerate((2, 1, 3, 0)):
        rows = lax.rem(x + dx, 4) * 256
        there = pg.at[pl.ds(pl.multiple_of((1 - core) * 1024 + rows, 256), 256)]
        here = from_core.at[pl.ds(pl.multiple_of(rows, 256), 256)]
        k = 0 if c == 0 else 62 + c
        swaps.append(remote(there, here, asend.at[k], arecv.at[k], twin))
        swaps[-1].start()

    spots = [(where[2 * f], lax.div(where[2 * f + 1], H)) for f in range(FRAMES)]

    def block(i, j):
        planes = []
        for p in range(2):
            total = None
            for f, (r, cb) in enumerate(spots):
                k = j - cb
                at = jnp.where((k < 0) | (k > 2), 0, jnp.clip(i * H - r, -H, FR) + H)
                k = jnp.clip(k, 0, 2)
                part = terms[f, p, k, pl.ds(at, H), :]
                total = part if total is None else total + part
            planes.append(total * inverse)
        return planes

    second = Exchange(out2, in2, relay2, send2, recv2)
    base = OUT_ROWS
    aside = []
    for n, (j, side) in enumerate(((0, -1), (5, 1))):
        at = base + n * HALF
        encode(out2, [at, at + H, at + 256, at + 256 + H], block(0, j) + block(5, j), at + 512)
        there = base + (1 - n) * HALF
        aside.append(
            remote(out2.at[pl.ds(at, HALF)], in2.at[pl.ds(there, HALF)], send2.at[10 + n], recv2.at[11 - n], dev(0, side))
        )
        aside[-1].start()
    for q in (3, 2):
        put_block(out2, q, block(5, 1 + COLUMNS[q]))
        put_block(out2, 4 + q, block(0, 1 + COLUMNS[q]))
        second.start(q)

    def piece_of(ref, k):
        return ref[k, :64, :].astype(F32) * tall(scales(ref[k, 64:, :]), 64)

    def put_piece(ref, k, value):
        largest = jnp.abs(value[:16])
        for t in range(16, 64, 16):
            largest = jnp.maximum(largest, jnp.abs(value[t : t + 16]))
        code = code_of(largest)
        ref[k, :64, :] = jnp.round(value * tall(scale_of(code), 64)).astype(jnp.int32).astype(I16)
        ref[k, 64:, :] = code.astype(jnp.int32).astype(I16)

    scatter = []
    for c, dx in enumerate((2, 1, 3, 0)):
        swaps[c].wait_recv()
        for dy in (2, 1, 3, 0):
            k = lax.rem(x + dx, 4) * 4 + lax.rem(y + dy, 4)
            rows = k * 64
            value = pg[pl.ds(pl.multiple_of(core * 1024 + rows, 64), 64), :] + from_core[pl.ds(pl.multiple_of(rows, 64), 64), :]
            d = dx * 4 + dy - 1
            if d < 0:
                half[...] = value
                continue
            put_piece(spread, d, value)
            scatter.append(remote(spread.at[d], pieces.at[d], asend.at[1 + d], arecv.at[1 + d], flat[d][0]))
            scatter[-1].start()

    put_strip(out2, 8, [block(i, 0) for i in range(1, 5)])
    second.lefts.start()
    put_strip(out2, 9, [block(i, 5) for i in range(1, 5)])
    second.rights.start()
    for n, (i, j) in enumerate(((0, 1), (0, 4), (5, 1), (5, 4))):
        planes = block(i, j)
        for p in range(2):
            edge[n, p] = planes[p]
    second.pass_on(3)
    second.pass_on(2)
    for n in range(2):
        aside[n].wait_recv()
    sums = {}
    for n, j in ((0, 1), (1, 4)):
        at = base + n * HALF
        scale = tall(scales(in2[at + 512 : at + 528, :]), H)
        for i, off, e in ((0, 0, n), (5, 256, 2 + n)):
            sums[(i, j)] = [edge[e, p] + in2[at + off + p * H : at + off + (p + 1) * H, :].astype(F32) * scale for p in range(2)]
    for q in (1, 0):
        put_block(out2, q, sums[(5, 1 + COLUMNS[q])])
        put_block(out2, 4 + q, sums[(0, 1 + COLUMNS[q])])
        second.start(q)

    for copy in scatter:
        copy.wait()
    total = half[...]
    for d in range(15):
        total = total + piece_of(pieces, d)
    put_piece(deep_all, deep, total)
    depth = []
    for d in (3, 2, 4, 1, 5, 0, 6):
        device = high[d]
        depth.append(remote(deep_all.at[deep], deep_all.at[deep], asend.at[16 + d], arecv.at[16 + d], device))
        depth[-1].start()

    for i in range(4):
        for j in range(4):
            planes = block(i + 1, j + 1)
            for p in range(2):
                stage[p, i * H : (i + 1) * H, j * H : (j + 1) * H] = win[p, j + 1, (i + 1) * H : (i + 2) * H, :] - planes[p]

    second.pass_on(1)
    for copy in depth:
        copy.wait()
    total = piece_of(deep_all, 0)
    for k in range(1, 8):
        total = total + piece_of(deep_all, k)
    put_piece(gathered, core * 16 + plane, total * (1.0 / 1024.0))
    gather = []
    mine = gathered.at[core * 16 + plane]
    by_hops = sorted(range(15), key=lambda d: -((0, 1, 2, 1)[(d + 1) // 4] + (0, 1, 2, 1)[(d + 1) % 4]))
    for d, (device, _, _) in enumerate(flat):
        gather.append(remote(mine, mine, asend.at[23 + d], arecv.at[23 + d], device))
    for d in by_hops:
        gather[d].start()
    cross = [remote(mine, mine, asend.at[38], arecv.at[38], twin)]
    cross[0].start()

    def take(k, spots):
        for (i, j), planes in open_blocks(in2, k, spots):
            for p in range(2):
                spot = (p, slice(i * H, (i + 1) * H), slice(j * H, (j + 1) * H))
                stage[spot] = stage[spot] - planes[p]

    for d in reversed(by_hops):
        gather[d].wait_recv()
        part = gathered.at[core * 16 + flat[d][2]]
        cross.append(remote(part, part, asend.at[48 + d], arecv.at[48 + d], twin))
        cross[-1].start()

    second.rights.wait_recv()
    take(8, [(i, 0) for i in range(4)])
    second.lefts.wait_recv()
    take(9, [(i, 3) for i in range(4)])
    for q in (3, 2, 1, 0):
        second.down[q].wait_recv()
        take(q, [(0, COLUMNS[q])])
        second.up[q].wait_recv()
        take(4 + q, [(3, COLUMNS[q])])

    def spell(own):
        for k in range(16):
            value = piece_of(gathered, own * 16 + k)
            q, h, part = k // 8, k // 4 % 2, k % 4
            grad_ref[own, q, part * 64 : part * 64 + 64, h * H : (h + 1) * H] = value

    spell(core)
    for copy in cross:
        copy.wait_recv()
    spell(1 - core)
    for copy in swaps:
        copy.wait_send()
    first.finish_sends()
    second.finish_sends()
    for copy in forwards + lends + aside + gather + cross:
        copy.wait_send()


def write_out(obj_ref, grad_ref, new_ref, out_ref, sems):
    copies = []
    for p in range(2):
        for k in range(2):
            rows = pl.ds(k * 256, 256)
            copies.append((obj_ref.at[p, rows], new_ref.at[p, rows]))
    for m in range(2):
        for q in range(2):
            copies.append((grad_ref.at[m, q], out_ref.at[m, q]))
    copies = [pltpu.make_async_copy(a, b, sems.at[k]) for k, (a, b) in enumerate(copies)]
    for copy in copies:
        copy.start()
    for copy in copies:
        copy.wait()


def tables():
    n = np.arange(FR)
    angles = (n[:, None] * n[None, :] % FR) * (2.0 * math.pi / FR)
    cosine, sine = np.cos(angles) / 16.0, np.sin(angles) / 16.0
    both = []
    for g in range(2):
        c, s = cosine[g::2, :H], sine[g::2, :H]
        both.append(np.block([[c, s], [-s, c]]))
    both = np.stack(both + [b.T for b in both])
    hi = both.astype(np.float32).astype(ml_dtypes.bfloat16)
    lo = (both - hi.astype(np.float64)).astype(np.float32).astype(ml_dtypes.bfloat16)
    order = np.zeros((FR, FR), np.float32)
    order[np.arange(FR), np.concatenate([n[0::2], n[1::2]])] = 1.0
    return hi, lo, np.stack([order, order.T]).astype(ml_dtypes.bfloat16)


def shards(object_field, probe, own_pos, own_amp, lend_pos, lend_live, recv_amp):
    sm = pl.BlockSpec(memory_space=pltpu.SMEM)
    hbm = pl.BlockSpec(memory_space=pl.ANY)
    dma = pltpu.SemaphoreType.DMA
    hi, lo, order = tables()

    def vm(shape, dtype=F32):
        return pltpu.VMEM(shape, dtype)

    args = (object_field, probe, own_pos.T, lend_pos, lend_live, own_amp, recv_amp, jnp.asarray(hi), jnp.asarray(lo), jnp.asarray(order))
    held = [pltpu.with_memory_space_constraint(a, pltpu.HBM) for a in args]
    new_object, probe_grad = pl.pallas_call(
        kernel,
        out_shape=(
            jax.ShapeDtypeStruct(object_field.shape, F32),
            jax.ShapeDtypeStruct(probe.shape, F32),
        ),
        in_specs=[hbm, hbm, sm, sm, sm, hbm, hbm, hbm, hbm, hbm],
        out_specs=(pl.BlockSpec(memory_space=pltpu.VMEM),) * 2,
        scratch_shapes=[
            vm((2, 6, WIN, H)),
            vm((2, 2, FR, FR)),
            vm((4, FR, FR), BF),
            vm((4, FR, FR), BF),
            vm((2, FR, FR), BF),
            vm((OWN, FR, FR), BF),
            vm((FRAMES - OWN, FR, FR), BF),
            vm((FRAMES, FR, FR), BF),
            vm((FRAMES, 2, 3, 2 * FR, H)),
            vm((2048, H)),
            pltpu.SMEM((2 * FRAMES,), jnp.int32),
            pltpu.SMEM((FRAMES,), F32),
            vm((OUT_ROWS, H), I16),
            vm((IN_ROWS, H), I16),
            vm((2, BLOCK, H), I16),
            vm((OUT_ROWS + 2 * HALF, H), I16),
            vm((OUT_ROWS + 2 * HALF, H), I16),
            vm((2, BLOCK, H), I16),
            vm((4, 2, H, H)),
            vm((1024, H)),
            vm((64, H)),
            vm((15, PIECE, H), I16),
            vm((15, PIECE, H), I16),
            vm((8, PIECE, H), I16),
            vm((32, PIECE, H), I16),
            dma((13,)),
            dma((16,)),
            dma((16,)),
            dma((16,)),
            dma((16,)),
            dma((66,)),
            dma((66,)),
        ],
        compiler_params=pltpu.CompilerParams(collective_id=0, has_side_effects=True, vmem_limit_bytes=46 << 20),
        name="step",
    )(*held)
    return pl.pallas_call(
        write_out,
        out_shape=(
            jax.ShapeDtypeStruct(object_field.shape, F32),
            jax.ShapeDtypeStruct(probe.shape, F32),
        ),
        in_specs=[pl.BlockSpec(memory_space=pltpu.VMEM)] * 2,
        out_specs=(hbm, hbm),
        scratch_shapes=[dma((8,))],
        compiler_params=pltpu.CompilerParams(vmem_limit_bytes=8 << 20),
        name="write_out",
    )(new_object, probe_grad)


def solution(mesh):
    placed = (
        P(None, "row", "col"),
        P(),
        P(("row", "col"), None),
        P(("row", "col"), None, None),
        P(("row", "col"), None),
        P(("row", "col")),
        P(("row", "col"), None, None),
    )
    return jax.shard_map(
        shards, mesh=mesh, in_specs=placed, out_specs=(P(None, "row", "col"), P()), check_vma=False
    )
```
